512 devices in a mesh: ctx: 16 (over y, core), dp: 32 (over z, x).
Axes of the slice: x: 4, y: 8, z: 8, core: 2. Of those that a mesh axis runs over, the one named last changes fastest.
Arguments:
- queries: bfloat16 [131072, 256], P(('dp', 'ctx')), parts along dimension 0, may hold values from -6 to 6
- key_states: bfloat16 [131072, 128], P(('dp', 'ctx')), parts along dimension 0, may hold values from -6 to 6
- value_states: bfloat16 [131072, 128], P(('dp', 'ctx')), parts along dimension 0, may hold values from -6 to 6
- attn_out: bfloat16 [131072, 256], P(('dp', 'ctx')), parts along dimension 0, may hold values from -0.59765625 to 0.59765625
- grad_out: bfloat16 [131072, 256], P(('dp', 'ctx')), parts along dimension 0, may hold values from -6 to 6
- log_norm: float32 [2, 131072], P(None, ('dp', 'ctx')), parts along dimension 1, may hold values from 1 to 4
- doc_lengths: int32 [128], P('dp'), parts along dimension 0, may hold values from 1 to 2048, 4096 in all
Outputs:
- grad_query: bfloat16 [131072, 256], P(('dp', 'ctx')), parts along dimension 0
- grad_key: bfloat16 [131072, 128], P(('dp', 'ctx')), parts along dimension 0
- grad_value: bfloat16 [131072, 128], P(('dp', 'ctx')), parts along dimension 0
The draws below stay inside these ranges and needn't reach their ends.
There are 32 independent parts, one for each index of `dp`. The reference program is written for one: setup_inputs(seed, part) draws one part's arguments, and reference() takes and returns one part's arrays. A program takes and returns all parts, laid end to end along the dimension named above; each array names one. Nothing has to cross between parts.
Inputs may be any that keep to these rules, and one draw needn't show every extreme that they name: `doc_lengths`: lengths of the documents packed in the sequence, in order of position; they sum to 4096 and the longest is exactly 2048.
All inputs are finite; a program needn't handle non-finite values.
Results may differ from the reference program's by a relative error of at most 0.0051.
Values may be sent and summed in bfloat16 or wider, within the bound.
No kernel may reach another device: no remote copies, remote signals or barrier semaphores. Data moves between devices by JAX's collectives and lax.ppermute only.
A program may use at most 64 MiB of HBM per device.

```python
import math
import jax
import jax.numpy as jnp
import numpy as np
from jax import lax

E = 128
H = 2
DOCS = 4
TOKENS = 4096
DOC_MAX = 2048


def level_of(rng, extent, split, low, top_value):
    factor_of, own = 1.0, jax.random.fold_in(rng, 6)
    for position, shards_of in split:
        heights = jnp.exp(jax.random.uniform(jax.random.fold_in(own, position), (shards_of,), jnp.float32, low / len(split), top_value / len(split)))
        factor_of = factor_of * jnp.repeat(heights, extent[position] // shards_of).reshape([-1 if axis == position else 1 for axis in range(len(extent))])
    return factor_of


def profile(number_of, total, limit, lean):
    loads = [(1 << 20) // math.isqrt(rank ** lean) + 1 for rank in range(2, number_of + 1)]
    rest, given = total - limit - (number_of - 1), [1] * (number_of - 1)
    while rest > 0:
        free = [i for i in range(number_of - 1) if given[i] < limit]
        pool, budget = sum([loads[i] for i in free]), rest
        for i in free:
            more = min(limit - given[i], max(1, budget * loads[i] // pool), rest)
            given[i] = given[i] + more
            rest = rest - more
    return np.array([limit] + given)


def ragged(rng, count, total, limit, skew):
    if count == 2:
        one = jax.random.randint(rng, (), max(1, total - limit), min(limit, total - 1) + 1)
        return jnp.stack([one, total - one])
    lengths = jnp.asarray(profile(count, total, limit, skew), jnp.int32)
    pairs = (count - 1) // 2
    donor, sink = lengths[1:1 + 2 * pairs:2], lengths[2:2 + 2 * pairs:2]
    room = jnp.minimum(donor - 1, limit - sink)
    moved = jax.random.randint(jax.random.fold_in(rng, 1), (pairs,), 0, 1 << 20) % (room + 1)
    lengths = lengths.at[1:1 + 2 * pairs:2].set(donor - moved).at[2:2 + 2 * pairs:2].set(sink + moved)
    return lengths[jax.random.permutation(jax.random.fold_in(rng, 2), count)]


def normal_values(own_key, shape, width, reach, pieces=(), kind=jnp.bfloat16):
    drawn = jax.random.normal(own_key, shape, jnp.float32) * width
    if len(pieces) > 0:
        drawn = level_of(own_key, shape, pieces, -0.22, 0.18) * drawn
    return jnp.clip(drawn, min=-reach, max=reach).astype(kind)


def setup_inputs(seed: int = 0, part: int = 0) -> dict:
    key_of = jax.random.split(jax.random.key(seed), 8)
    part_splits = jax.random.split(jax.random.fold_in(key_of[7], part), 8)
    return {
        "queries": normal_values(part_splits[0], (TOKENS, H * E), 1.0, 6.0, ((0, 16),)),
        "key_states": normal_values(part_splits[1], (TOKENS, E), 1.0, 6.0, ((0, 16),)),
        "value_states": normal_values(part_splits[2], (TOKENS, E), 1.0, 6.0, ((0, 16),)),
        "attn_out": normal_values(part_splits[3], (TOKENS, H * E), 0.1, 0.59765625, ((0, 16),)),
        "grad_out": normal_values(part_splits[4], (TOKENS, H * E), 1.0, 6.0, ((0, 16),)),
        "log_norm": jnp.clip(1.0 + 3.0 * jax.random.uniform(part_splits[5], (H, TOKENS), jnp.float32) ** level_of(part_splits[5], (H, TOKENS), ((1, 16),), -0.2, 0.2), 1.0, 4.0),
        "doc_lengths": ragged(part_splits[6], DOCS, TOKENS, DOC_MAX, 2).astype(jnp.int32),
    }


def doc_index(doc_ends, positions):
    return jnp.sum((doc_ends[None, :] <= positions[:, None]).astype(jnp.int32), axis=1)


def tile_grads(queries, grad_out, log_norm, row_delta, q_pos, key_states, value_states, k_pos, doc_ends):
    q_count = queries.shape[0]
    head_count = log_norm.shape[0]
    head_dim = key_states.shape[1]
    scaling = head_dim ** -0.5
    query_heads = queries.reshape(q_count, head_count, head_dim).astype(jnp.float32)
    grad_heads = grad_out.reshape(q_count, head_count, head_dim).astype(jnp.float32)
    scores = jnp.einsum("qhe,ke->hqk", query_heads, key_states.astype(jnp.float32)) * scaling
    allowed = (doc_index(doc_ends, q_pos)[:, None] == doc_index(doc_ends, k_pos)[None, :]) & (k_pos[None, :] <= q_pos[:, None])
    attn_prob = jnp.where(allowed[None], jnp.exp(scores - log_norm[:, :, None]), 0.0)
    grad_prob = jnp.einsum("qhe,ke->hqk", grad_heads, value_states.astype(jnp.float32))
    dscore = (attn_prob * (grad_prob - row_delta[:, :, None]) * scaling).astype(jnp.bfloat16)
    return dscore, attn_prob.astype(jnp.bfloat16), query_heads, grad_heads


def reference(queries, key_states, value_states, attn_out, grad_out, log_norm, doc_lengths):
    seq_len, head_dim = key_states.shape
    head_count = log_norm.shape[0]
    doc_ends = jnp.cumsum(doc_lengths).astype(jnp.int32)
    positions = jnp.arange(seq_len, dtype=jnp.int32)
    row_delta = jnp.sum((grad_out.astype(jnp.float32) * attn_out.astype(jnp.float32)).reshape(seq_len, head_count, head_dim), axis=2).T
    block_len = math.gcd(seq_len, 512)

    def one_block(running, block_id):
        first_row = (block_id * block_len).astype(jnp.int32)
        query_slab = lax.dynamic_slice_in_dim(queries, first_row, block_len, 0)
        grad_slab = lax.dynamic_slice_in_dim(grad_out, first_row, block_len, 0)
        stats_slab = lax.dynamic_slice_in_dim(log_norm, first_row, block_len, 1)
        delta_slab = lax.dynamic_slice_in_dim(row_delta, first_row, block_len, 1)
        query_pos = first_row + jnp.arange(block_len, dtype=jnp.int32)
        dscore, prob_half, query_heads, grad_heads = tile_grads(query_slab, grad_slab, stats_slab, delta_slab, query_pos, key_states, value_states, positions, doc_ends)
        dscore_wide = dscore.astype(jnp.float32)
        grad_rows = jnp.einsum("hqk,ke->qhe", dscore_wide, key_states.astype(jnp.float32))
        grad_keys = running[0] + jnp.einsum("hqk,qhe->ke", dscore_wide, query_heads)
        grad_values = running[1] + jnp.einsum("hqk,qhe->ke", prob_half.astype(jnp.float32), grad_heads)
        return (grad_keys, grad_values), grad_rows.reshape(block_len, head_count * head_dim).astype(jnp.bfloat16)

    zero_grads = jnp.zeros((seq_len, head_dim), jnp.float32)
    finals, grad_rows = lax.scan(one_block, (zero_grads, zero_grads), jnp.arange(seq_len // block_len, dtype=jnp.int32))
    grad_query = grad_rows.reshape(seq_len, head_count * head_dim)
    return grad_query, finals[0].astype(jnp.bfloat16), finals[1].astype(jnp.bfloat16)
```

```python
import functools
import math

import jax
import jax.numpy as jnp
from jax import lax
from jax.experimental import pallas as pl
from jax.experimental.pallas import tpu as pltpu
from jax.sharding import PartitionSpec as P

LOG2E = math.log2(math.e)
STAT_ROWS = 16


def split3(value):
    high = value.astype(jnp.bfloat16)
    rest = value - high.astype(jnp.float32)
    mid = rest.astype(jnp.bfloat16)
    low = (rest - mid.astype(jnp.float32)).astype(jnp.bfloat16)
    return high, mid, low


def prep_kernel(q_ref, go_ref, out_ref, norm_ref, k_ref, v_ref, pay_ref, kv_ref):
    rows, width = q_ref.shape
    heads = norm_ref.shape[0]
    head_dim = width // heads
    kv_ref[:, :head_dim] = k_ref[...]
    kv_ref[:, head_dim:] = v_ref[...]
    pay_ref[:rows, :width] = q_ref[...]
    pay_ref[:rows, width:] = go_ref[...]
    product = go_ref[...].astype(jnp.float32) * out_ref[...].astype(jnp.float32)
    product_t = product.T
    stats = []
    for h in range(heads):
        delta = jnp.sum(product_t[h * head_dim : (h + 1) * head_dim], axis=0, keepdims=True)
        stats += list(split3(norm_ref[h : h + 1, :] * LOG2E)) + list(split3(delta))
    stats += [jnp.zeros((1, rows), jnp.bfloat16)] * (STAT_ROWS - len(stats))
    table = jnp.concatenate([s.astype(jnp.float32) for s in stats], axis=0)
    pay_ref[rows:, :rows] = table.astype(jnp.bfloat16)
    pay_ref[rows:, rows:] = jnp.zeros((STAT_ROWS, pay_ref.shape[1] - rows), jnp.bfloat16)


class Query:
    def __init__(self, pay_ref, heads, first, lens_ref):
        rows = pay_ref.shape[0] - STAT_ROWS
        width = pay_ref.shape[1] // 2
        e = width // heads
        self.heads, self.rows, self.e = heads, rows, e
        self.q = [pay_ref[:rows, h * e : (h + 1) * e] for h in range(heads)]
        self.go = [pay_ref[:rows, width + h * e : width + (h + 1) * e] for h in range(heads)]
        table = pay_ref[rows:, :rows].astype(jnp.float32)
        row = lambda i: table[i : i + 1]
        self.norm = [row(6 * h) + row(6 * h + 1) + row(6 * h + 2) for h in range(heads)]
        self.delta = [row(6 * h + 3) + row(6 * h + 4) + row(6 * h + 5) for h in range(heads)]
        self.pos = first + lax.broadcasted_iota(jnp.int32, (1, rows), 1)
        self.start = jnp.zeros((1, rows), jnp.int32)
        end = jnp.int32(0)
        for d in range(lens_ref.shape[0]):
            end = end + lens_ref[d]
            self.start = jnp.where(end <= self.pos, end, self.start)


def tile(query, h, k_block, v_block, k_first, causal):
    contract = (((1,), (1,)), ((), ()))
    scaling = query.e ** (-0.5)
    scores = lax.dot_general(k_block, query.q[h], contract, preferred_element_type=jnp.float32)
    grads = lax.dot_general(v_block, query.go[h], contract, preferred_element_type=jnp.float32)
    k_pos = k_first + lax.broadcasted_iota(jnp.int32, (k_block.shape[0], 1), 0)
    allowed = k_pos >= query.start
    if causal:
        allowed = allowed & (k_pos <= query.pos)
    prob = jnp.where(allowed, jnp.exp2(scores * (scaling * LOG2E) - query.norm[h]), 0.0)
    dscore = (prob * (grads - query.delta[h]) * scaling).astype(jnp.bfloat16)
    return prob.astype(jnp.bfloat16), dscore


def key_terms(query, k_block, v_block, k_first, causal, dqt):
    dk = dv = None
    for h in range(query.heads):
        prob, dscore = tile(query, h, k_block, v_block, k_first, causal)
        dv_h = jnp.dot(prob, query.go[h], preferred_element_type=jnp.float32)
        dk_h = jnp.dot(dscore, query.q[h], preferred_element_type=jnp.float32)
        dv = dv_h if dv is None else dv + dv_h
        dk = dk_h if dk is None else dk + dk_h
        dq_h = lax.dot_general(
            k_block, dscore, (((0,), (0,)), ((), ())), preferred_element_type=jnp.float32
        )
        dqt[h] = dq_h if dqt[h] is None else dqt[h] + dq_h
    return dk, dv


def place():
    index = lax.axis_index("ctx")
    return index, index // 2, lax.rem(index, 2)


def block_start(chip, back, chips, rows):
    behind = chip - back
    return jnp.where(behind >= 0, behind, -2 * chips) * (2 * rows)


def own_kernel(heads, lens_ref, pay_ref, kv_ref, dqt_ref, keep_ref, give_ref):
    rows = pay_ref.shape[0] - STAT_ROWS
    e = kv_ref.shape[1] // 2
    index, chip, core = place()
    query = Query(pay_ref, heads, index * rows, lens_ref)
    dqt = [None] * heads
    for half in range(2):
        part = pl.ds(half * rows, rows)
        dk, dv = key_terms(
            query, kv_ref[part, :e], kv_ref[part, e:], (2 * chip + half) * rows, True, dqt
        )

        @pl.when(core == half)
        def _():
            keep_ref[:, :e] = dk
            keep_ref[:, e:] = dv

        @pl.when(core != half)
        def _():
            give_ref[:, :e] = dk
            give_ref[:, e:] = dv

    for h in range(heads):
        dqt_ref[h * e : (h + 1) * e, :] = dqt[h]


def near_kernel(heads, chips, lens_ref, pay_ref, kv_ref, dqt_in_ref, dqt_ref, terms_ref):
    rows = pay_ref.shape[0] - STAT_ROWS
    e = kv_ref.shape[1] // 2
    index, chip, core = place()
    query = Query(pay_ref, heads, index * rows, lens_ref)
    dqt = [dqt_in_ref[h * e : (h + 1) * e, :] for h in range(heads)]
    for half in range(2):
        for b in range(2):
            part = pl.ds((half * 2 + b) * rows, rows)
            first = block_start(chip, b + 1, chips, rows) + half * rows
            dk, dv = key_terms(query, kv_ref[part, :e], kv_ref[part, e:], first, False, dqt)
            terms_ref[part, :e] = dk
            terms_ref[part, e:] = dv
    for h in range(heads):
        dqt_ref[h * e : (h + 1) * e, :] = dqt[h]


def far_kernel(heads, chips, lens_ref, pay_ref, kv_ref, terms_ref, dqt_ref, keep_ref, give_ref):
    rows = pay_ref.shape[0] - STAT_ROWS
    e = kv_ref.shape[1] // 2
    index, chip, core = place()
    ahead = chip + 2
    query = Query(pay_ref, heads, (index + 4) * rows, lens_ref)
    query.start = jnp.where(ahead < chips, query.start, 4 * chips * rows)
    dqt = [None] * heads
    for half in range(2):
        for b in range(2):
            part = pl.ds((half * 2 + b) * rows, rows)
            first = block_start(chip, b + 1, chips, rows) + half * rows
            dk, dv = key_terms(query, kv_ref[part, :e], kv_ref[part, e:], first, False, dqt)
            dk = dk + terms_ref[part, :e]
            dv = dv + terms_ref[part, e:]
            out = pl.ds(b * rows, rows)

            @pl.when(core == half)
            def _():
                keep_ref[out, :e] = dk
                keep_ref[out, e:] = dv

            @pl.when(core != half)
            def _():
                give_ref[out, :e] = dk
                give_ref[out, e:] = dv

    for h in range(heads):
        dqt_ref[h * e : (h + 1) * e, :] = dqt[h].astype(jnp.bfloat16)


def pair_kernel(keep_ref, both_ref, near_ref, far_ref):
    count = keep_ref.shape[0]
    rows = count // 2
    _, _, core = place()
    other = both_ref[pl.ds(pl.multiple_of((1 - core) * count, count), count), :]
    total = (keep_ref[...] + other).astype(jnp.bfloat16)
    near_ref[...] = total[:rows]
    far_ref[...] = total[rows:]


def query_kernel(dqt_ref, back_ref, dq_ref):
    dq_ref[...] = (dqt_ref[...] + back_ref[...].astype(jnp.float32)).T.astype(jnp.bfloat16)


def key_kernel(keep_ref, both_ref, near_ref, far_ref, dk_ref, dv_ref):
    rows = keep_ref.shape[0]
    e = keep_ref.shape[1] // 2
    _, _, core = place()
    other = both_ref[pl.ds(pl.multiple_of((1 - core) * rows, rows), rows), :]
    total = keep_ref[...] + other
    total = total + near_ref[...].astype(jnp.float32) + far_ref[...].astype(jnp.float32)
    dk_ref[...] = total[:, :e].astype(jnp.bfloat16)
    dv_ref[...] = total[:, e:].astype(jnp.bfloat16)


def call(kernel, outs, name, flops=0, smem=0):
    def run(*args):
        specs = [pl.BlockSpec(memory_space=pltpu.SMEM)] * smem
        specs += [pl.BlockSpec(memory_space=pltpu.VMEM)] * (len(args) - smem)
        moved = sum(a.size * a.dtype.itemsize for a in args)
        return pl.pallas_call(
            kernel,
            out_shape=[jax.ShapeDtypeStruct(s, d) for s, d in outs],
            in_specs=specs,
            out_specs=[pl.BlockSpec(memory_space=pltpu.VMEM)] * len(outs),
            cost_estimate=pl.CostEstimate(flops=flops, bytes_accessed=moved, transcendentals=0),
            compiler_params=pltpu.CompilerParams(vmem_limit_bytes=32 * 1024 * 1024),
            name=name,
        )(*args)

    return run


def body(queries, key_states, value_states, attn_out, grad_out, log_norm, doc_lengths):
    rows, width = queries.shape
    heads = log_norm.shape[0]
    e = key_states.shape[1]
    count = lax.axis_size("ctx")
    chips = count // 2
    pairs = [[2 * i, 2 * i + 1] for i in range(chips)]
    bf16, f32 = jnp.bfloat16, jnp.float32

    def shift(x, by):
        return lax.ppermute(x, "ctx", [(i, (i + by) % count) for i in range(count)])

    def pair_gather(x):
        return lax.all_gather(x, "ctx", axis=0, tiled=True, axis_index_groups=pairs)

    pay, kv = call(
        prep_kernel, [((rows + STAT_ROWS, 2 * width), bf16), ((rows, 2 * e), bf16)], "prep"
    )(queries, grad_out, attn_out, log_norm, key_states, value_states)
    pay_far = shift(pay, -4)
    kv_far = shift(kv, 4)
    kv_near = shift(kv, 2)
    kv_own = pair_gather(kv)
    unit = 5 * 2 * heads * rows * 2 * rows * e
    dqt, keep_own, give_own = call(
        functools.partial(own_kernel, heads),
        [((width, rows), f32), ((rows, 2 * e), f32), ((rows, 2 * e), f32)],
        "own",
        unit,
        1,
    )(doc_lengths, pay, kv_own)
    kv_back = pair_gather(jnp.concatenate([kv_near, kv_far], axis=0))
    dqt, terms = call(
        functools.partial(near_kernel, heads, chips),
        [((width, rows), f32), ((4 * rows, 2 * e), f32)],
        "near",
        2 * unit,
        1,
    )(doc_lengths, pay, kv_back, dqt)
    dqt_far, keep, give = call(
        functools.partial(far_kernel, heads, chips),
        [((width, rows), bf16), ((2 * rows, 2 * e), f32), ((2 * rows, 2 * e), f32)],
        "far",
        2 * unit,
        1,
    )(doc_lengths, pay_far, kv_back, terms)
    dqt_back = shift(dqt_far, 4)
    both = pair_gather(give)
    to_near, to_far = call(
        pair_kernel, [((rows, 2 * e), bf16), ((rows, 2 * e), bf16)], "pair"
    )(keep, both)
    from_far = shift(to_far, -4)
    from_near = shift(to_near, -2)
    both_own = pair_gather(give_own)
    (grad_query,) = call(query_kernel, [((rows, width), bf16)], "grad_query")(dqt, dqt_back)
    grad_key, grad_value = call(
        key_kernel, [((rows, e), bf16), ((rows, e), bf16)], "grad_key"
    )(keep_own, both_own, from_near, from_far)
    return (grad_query, grad_key, grad_value)


def solution(mesh):
    rows = P(("dp", "ctx"), None)
    placed = (rows, rows, rows, rows, rows, P(None, ("dp", "ctx")), P("dp"))
    return jax.shard_map(
        body, mesh=mesh, in_specs=placed, out_specs=(rows, rows, rows), check_vma=False
    )
```

```python
import functools
import math

import jax
import jax.numpy as jnp
from jax import lax
from jax.experimental import pallas as pl
from jax.experimental.pallas import tpu as pltpu
from jax.sharding import PartitionSpec as P

LOG2E = math.log2(math.e)
STAT_ROWS = 16


def split3(value):
    high = value.astype(jnp.bfloat16)
    rest = value - high.astype(jnp.float32)
    mid = rest.astype(jnp.bfloat16)
    low = (rest - mid.astype(jnp.float32)).astype(jnp.bfloat16)
    return high, mid, low


def prep_kernel(q_ref, go_ref, out_ref, norm_ref, k_ref, v_ref, pay_ref, kv_ref, *scratch):
    out_buf, norm_buf, sems = scratch
    rows, width = q_ref.shape
    heads = norm_ref.shape[0]
    e = width // heads
    moves = [
        (go_ref, pay_ref.at[:rows, width:]),
        (out_ref, out_buf),
        (norm_ref, norm_buf),
        (q_ref, pay_ref.at[:rows, :width]),
        (k_ref, kv_ref.at[:, :e]),
        (v_ref, kv_ref.at[:, e:]),
    ]
    copies = [pltpu.make_async_copy(s, d, sems.at[i]) for i, (s, d) in enumerate(moves)]
    for copy in copies:
        copy.start()
    for copy in copies[:3]:
        copy.wait()
    product = pay_ref[:rows, width:].astype(jnp.float32) * out_buf[...].astype(jnp.float32)
    product_t = product.T
    stats = []
    for h in range(heads):
        delta = jnp.sum(product_t[h * e : (h + 1) * e], axis=0, keepdims=True)
        stats += list(split3(norm_buf[h : h + 1, :] * LOG2E)) + list(split3(delta))
    stats += [jnp.zeros((1, rows), jnp.bfloat16)] * (STAT_ROWS - len(stats))
    table = jnp.concatenate([s.astype(jnp.float32) for s in stats], axis=0)
    pay_ref[rows:, :rows] = table.astype(jnp.bfloat16)
    pay_ref[rows:, rows:] = jnp.zeros((STAT_ROWS, pay_ref.shape[1] - rows), jnp.bfloat16)
    for copy in copies[3:]:
        copy.wait()


class Query:
    def __init__(self, pay_ref, heads, first, lens_ref):
        rows = pay_ref.shape[0] - STAT_ROWS
        width = pay_ref.shape[1] // 2
        e = width // heads
        self.heads, self.rows, self.e = heads, rows, e
        self.q = [pay_ref[:rows, h * e : (h + 1) * e] for h in range(heads)]
        self.go = [pay_ref[:rows, width + h * e : width + (h + 1) * e] for h in range(heads)]
        table = pay_ref[rows:, :rows].astype(jnp.float32)
        row = lambda i: table[i : i + 1]
        self.norm = [row(6 * h) + row(6 * h + 1) + row(6 * h + 2) for h in range(heads)]
        self.delta = [row(6 * h + 3) + row(6 * h + 4) + row(6 * h + 5) for h in range(heads)]
        self.pos = first + lax.broadcasted_iota(jnp.int32, (1, rows), 1)
        self.start = jnp.zeros((1, rows), jnp.int32)
        end = jnp.int32(0)
        for d in range(lens_ref.shape[0]):
            end = end + lens_ref[d]
            self.start = jnp.where(end <= self.pos, end, self.start)


def tile(query, h, k_block, v_block, k_first, causal):
    contract = (((1,), (1,)), ((), ()))
    scaling = query.e ** (-0.5)
    scores = lax.dot_general(k_block, query.q[h], contract, preferred_element_type=jnp.float32)
    grads = lax.dot_general(v_block, query.go[h], contract, preferred_element_type=jnp.float32)
    k_pos = k_first + lax.broadcasted_iota(jnp.int32, (k_block.shape[0], 1), 0)
    allowed = k_pos >= query.start
    if causal:
        allowed = allowed & (k_pos <= query.pos)
    prob = jnp.where(allowed, jnp.exp2(scores * (scaling * LOG2E) - query.norm[h]), 0.0)
    dscore = (prob * (grads - query.delta[h]) * scaling).astype(jnp.bfloat16)
    return prob.astype(jnp.bfloat16), dscore


def key_terms(query, k_block, v_block, k_first, causal, dqt):
    dk = dv = None
    for h in range(query.heads):
        prob, dscore = tile(query, h, k_block, v_block, k_first, causal)
        dv_h = jnp.dot(prob, query.go[h], preferred_element_type=jnp.float32)
        dk_h = jnp.dot(dscore, query.q[h], preferred_element_type=jnp.float32)
        dv = dv_h if dv is None else dv + dv_h
        dk = dk_h if dk is None else dk + dk_h
        dq_h = lax.dot_general(
            k_block, dscore, (((0,), (0,)), ((), ())), preferred_element_type=jnp.float32
        )
        dqt[h] = dq_h if dqt[h] is None else dqt[h] + dq_h
    return dk, dv


def place():
    index = lax.axis_index("ctx")
    return index, index // 2, lax.rem(index, 2)


def block_start(chip, back, chips, rows):
    behind = chip - back
    return jnp.where(behind >= 0, behind, -2 * chips) * (2 * rows)


def own_kernel(heads, lens_ref, pay_ref, kv_ref, dqt_ref, keep_ref, give_ref):
    rows = pay_ref.shape[0] - STAT_ROWS
    e = kv_ref.shape[1] // 2
    index, chip, core = place()
    query = Query(pay_ref, heads, index * rows, lens_ref)
    dqt = [None] * heads
    for half in range(2):
        part = pl.ds(half * rows, rows)
        dk, dv = key_terms(
            query, kv_ref[part, :e], kv_ref[part, e:], (2 * chip + half) * rows, True, dqt
        )

        @pl.when(core == half)
        def _():
            keep_ref[:, :e] = dk
            keep_ref[:, e:] = dv

        @pl.when(core != half)
        def _():
            give_ref[:, :e] = dk
            give_ref[:, e:] = dv

    for h in range(heads):
        dqt_ref[h * e : (h + 1) * e, :] = dqt[h]


def near_kernel(heads, chips, lens_ref, pay_ref, kv_ref, dqt_in_ref, dqt_ref, terms_ref):
    rows = pay_ref.shape[0] - STAT_ROWS
    e = kv_ref.shape[1] // 2
    index, chip, core = place()
    query = Query(pay_ref, heads, index * rows, lens_ref)
    dqt = [dqt_in_ref[h * e : (h + 1) * e, :] for h in range(heads)]
    for half in range(2):
        for b in range(2):
            part = pl.ds((half * 2 + b) * rows, rows)
            first = block_start(chip, b + 1, chips, rows) + half * rows
            dk, dv = key_terms(query, kv_ref[part, :e], kv_ref[part, e:], first, False, dqt)
            terms_ref[part, :e] = dk
            terms_ref[part, e:] = dv
    for h in range(heads):
        dqt_ref[h * e : (h + 1) * e, :] = dqt[h]


def far_kernel(heads, chips, lens_ref, pay_ref, kv_ref, terms_ref, dqt_ref, keep_ref, give_ref):
    rows = pay_ref.shape[0] - STAT_ROWS
    e = kv_ref.shape[1] // 2
    index, chip, core = place()
    ahead = chip + 2
    query = Query(pay_ref, heads, (index + 4) * rows, lens_ref)
    query.start = jnp.where(ahead < chips, query.start, 4 * chips * rows)
    dqt = [None] * heads
    for half in range(2):
        for b in range(2):
            part = pl.ds((half * 2 + b) * rows, rows)
            first = block_start(chip, b + 1, chips, rows) + half * rows
            dk, dv = key_terms(query, kv_ref[part, :e], kv_ref[part, e:], first, False, dqt)
            dk = dk + terms_ref[part, :e]
            dv = dv + terms_ref[part, e:]
            out = pl.ds(b * rows, rows)

            @pl.when(core == half)
            def _():
                keep_ref[out, :e] = dk
                keep_ref[out, e:] = dv

            @pl.when(core != half)
            def _():
                give_ref[out, :e] = dk.astype(jnp.bfloat16)
                give_ref[out, e:] = dv.astype(jnp.bfloat16)

    for h in range(heads):
        dqt_ref[h * e : (h + 1) * e, :] = dqt[h].astype(jnp.bfloat16)


def pair_kernel(keep_ref, both_ref, near_ref, far_ref):
    count = keep_ref.shape[0]
    rows = count // 2
    _, _, core = place()
    other = both_ref[pl.ds(pl.multiple_of((1 - core) * count, count), count), :]
    total = (keep_ref[...] + other.astype(jnp.float32)).astype(jnp.bfloat16)
    near_ref[...] = total[:rows]
    far_ref[...] = total[rows:]


def query_kernel(dqt_ref, back_ref, dq_ref):
    dq_ref[...] = (dqt_ref[...] + back_ref[...].astype(jnp.float32)).T.astype(jnp.bfloat16)


def key_kernel(keep_ref, both_ref, near_ref, far_ref, dk_ref, dv_ref):
    rows = keep_ref.shape[0]
    e = keep_ref.shape[1] // 2
    _, _, core = place()
    other = both_ref[pl.ds(pl.multiple_of((1 - core) * rows, rows), rows), :]
    total = keep_ref[...] + other
    total = total + near_ref[...].astype(jnp.float32) + far_ref[...].astype(jnp.float32)
    dk_ref[...] = total[:, :e].astype(jnp.bfloat16)
    dv_ref[...] = total[:, e:].astype(jnp.bfloat16)


def call(kernel, outs, name, flops=0, smem=0, space=pltpu.VMEM, scratch=()):
    def run(*args):
        specs = [pl.BlockSpec(memory_space=pltpu.SMEM)] * smem
        specs += [pl.BlockSpec(memory_space=space)] * (len(args) - smem)
        moved = sum(a.size * a.dtype.itemsize for a in args)
        return pl.pallas_call(
            kernel,
            out_shape=[jax.ShapeDtypeStruct(s, d) for s, d in outs],
            in_specs=specs,
            out_specs=[pl.BlockSpec(memory_space=pltpu.VMEM)] * len(outs),
            scratch_shapes=list(scratch),
            cost_estimate=pl.CostEstimate(flops=flops, bytes_accessed=moved, transcendentals=0),
            compiler_params=pltpu.CompilerParams(vmem_limit_bytes=32 * 1024 * 1024),
            name=name,
        )(*args)

    return run


def body(queries, key_states, value_states, attn_out, grad_out, log_norm, doc_lengths):
    rows, width = queries.shape
    heads = log_norm.shape[0]
    e = key_states.shape[1]
    count = lax.axis_size("ctx")
    chips = count // 2
    pairs = [[2 * i, 2 * i + 1] for i in range(chips)]
    bf16, f32 = jnp.bfloat16, jnp.float32

    def shift(x, by):
        return lax.ppermute(x, "ctx", [(i, (i + by) % count) for i in range(count)])

    def pair_gather(x):
        return lax.all_gather(x, "ctx", axis=0, tiled=True, axis_index_groups=pairs)

    pay, kv = call(
        prep_kernel,
        [((rows + STAT_ROWS, 2 * width), bf16), ((rows, 2 * e), bf16)],
        "prep",
        space=pltpu.HBM,
        scratch=[
            pltpu.VMEM((rows, width), bf16),
            pltpu.VMEM((heads, rows), f32),
            pltpu.SemaphoreType.DMA((6,)),
        ],
    )(
        *[
            pltpu.with_memory_space_constraint(x, pltpu.HBM)
            for x in (queries, grad_out, attn_out, log_norm, key_states, value_states)
        ]
    )
    pay_far = shift(pay, -4)
    kv_far = shift(kv, 4)
    kv_near = shift(kv, 2)
    kv_own = pair_gather(kv)
    unit = 5 * 2 * heads * rows * 2 * rows * e
    dqt, keep_own, give_own = call(
        functools.partial(own_kernel, heads),
        [((width, rows), f32), ((rows, 2 * e), f32), ((rows, 2 * e), f32)],
        "own",
        unit,
        1,
    )(doc_lengths, pay, kv_own)
    kv_back = pair_gather(jnp.concatenate([kv_near, kv_far], axis=0))
    dqt, terms = call(
        functools.partial(near_kernel, heads, chips),
        [((width, rows), f32), ((4 * rows, 2 * e), f32)],
        "near",
        2 * unit,
        1,
    )(doc_lengths, pay, kv_back, dqt)
    dqt_far, keep, give = call(
        functools.partial(far_kernel, heads, chips),
        [((width, rows), bf16), ((2 * rows, 2 * e), f32), ((2 * rows, 2 * e), bf16)],
        "far",
        2 * unit,
        1,
    )(doc_lengths, pay_far, kv_back, terms)
    dqt_back = shift(dqt_far, 4)
    both = pair_gather(give)
    to_near, to_far = call(
        pair_kernel, [((rows, 2 * e), bf16), ((rows, 2 * e), bf16)], "pair"
    )(keep, both)
    from_far = shift(to_far, -4)
    from_near = shift(to_near, -2)
    both_own = pair_gather(give_own)
    (grad_query,) = call(query_kernel, [((rows, width), bf16)], "grad_query")(dqt, dqt_back)
    grad_key, grad_value = call(
        key_kernel, [((rows, e), bf16), ((rows, e), bf16)], "grad_key"
    )(keep_own, both_own, from_near, from_far)
    return (grad_query, grad_key, grad_value)


def solution(mesh):
    rows = P(("dp", "ctx"), None)
    placed = (rows, rows, rows, rows, rows, P(None, ("dp", "ctx")), P("dp"))
    return jax.shard_map(
        body, mesh=mesh, in_specs=placed, out_specs=(rows, rows, rows), check_vma=False
    )
```

```python
import functools
import math

import jax
import jax.numpy as jnp
from jax import lax
from jax.experimental import pallas as pl
from jax.experimental.pallas import tpu as pltpu
from jax.sharding import PartitionSpec as P

LOG2E = math.log2(math.e)
STAT_ROWS = 16


def split3(value):
    high = value.astype(jnp.bfloat16)
    rest = value - high.astype(jnp.float32)
    mid = rest.astype(jnp.bfloat16)
    low = (rest - mid.astype(jnp.float32)).astype(jnp.bfloat16)
    return high, mid, low


def prep_kernel(q_ref, go_ref, out_ref, norm_ref, k_ref, v_ref, pay_ref, kv_ref, *scratch):
    out_buf, norm_buf, sems = scratch
    rows, width = q_ref.shape
    heads = norm_ref.shape[0]
    e = width // heads
    moves = [
        (go_ref, pay_ref.at[:rows, width:]),
        (out_ref, out_buf),
        (norm_ref, norm_buf),
        (q_ref, pay_ref.at[:rows, :width]),
        (k_ref, kv_ref.at[:, :e]),
        (v_ref, kv_ref.at[:, e:]),
    ]
    copies = [pltpu.make_async_copy(s, d, sems.at[i]) for i, (s, d) in enumerate(moves)]
    for copy in copies:
        copy.start()
    for copy in copies[:3]:
        copy.wait()
    product = pay_ref[:rows, width:].astype(jnp.float32) * out_buf[...].astype(jnp.float32)
    product_t = product.T
    stats = []
    for h in range(heads):
        delta = jnp.sum(product_t[h * e : (h + 1) * e], axis=0, keepdims=True)
        stats += list(split3(norm_buf[h : h + 1, :] * LOG2E)) + list(split3(delta))
    stats += [jnp.zeros((1, rows), jnp.bfloat16)] * (STAT_ROWS - len(stats))
    table = jnp.concatenate([s.astype(jnp.float32) for s in stats], axis=0)
    pay_ref[rows:, :rows] = table.astype(jnp.bfloat16)
    pay_ref[rows:, rows:] = jnp.zeros((STAT_ROWS, pay_ref.shape[1] - rows), jnp.bfloat16)
    for copy in copies[3:]:
        copy.wait()


class Query:
    def __init__(self, pay_ref, heads, first, lens_ref):
        rows = pay_ref.shape[0] - STAT_ROWS
        width = pay_ref.shape[1] // 2
        e = width // heads
        self.heads, self.rows, self.e = heads, rows, e
        self.q = [pay_ref[:rows, h * e : (h + 1) * e] for h in range(heads)]
        self.go = [pay_ref[:rows, width + h * e : width + (h + 1) * e] for h in range(heads)]
        table = pay_ref[rows:, :rows].astype(jnp.float32)
        row = lambda i: table[i : i + 1]
        self.norm = [row(6 * h) + row(6 * h + 1) + row(6 * h + 2) for h in range(heads)]
        self.delta = [row(6 * h + 3) + row(6 * h + 4) + row(6 * h + 5) for h in range(heads)]
        self.pos = first + lax.broadcasted_iota(jnp.int32, (1, rows), 1)
        self.start = jnp.zeros((1, rows), jnp.int32)
        end = jnp.int32(0)
        for d in range(lens_ref.shape[0]):
            end = end + lens_ref[d]
            self.start = jnp.where(end <= self.pos, end, self.start)


def scores_block(query, h, k_block, v_block, k_first, causal):
    contract = (((1,), (1,)), ((), ()))
    scaling = query.e ** (-0.5)
    scores = lax.dot_general(k_block, query.q[h], contract, preferred_element_type=jnp.float32)
    grads = lax.dot_general(v_block, query.go[h], contract, preferred_element_type=jnp.float32)
    k_pos = k_first + lax.broadcasted_iota(jnp.int32, (k_block.shape[0], 1), 0)
    allowed = k_pos >= query.start
    if causal:
        allowed = allowed & (k_pos <= query.pos)
    prob = jnp.where(allowed, jnp.exp2(scores * (scaling * LOG2E) - query.norm[h]), 0.0)
    dscore = prob * (grads - query.delta[h]) * scaling
    return prob.astype(jnp.bfloat16), dscore.astype(jnp.bfloat16)


def fill(queries, kv_ref, firsts, causal, prob_ref, dscore_ref):
    e = kv_ref.shape[1] // 2
    rows = kv_ref.shape[0] // len(firsts)
    for block, first in enumerate(firsts):
        part = pl.ds(block * rows, rows)
        k_block, v_block = kv_ref[part, :e], kv_ref[part, e:]
        column = 0
        for query in queries:
            for h in range(query.heads):
                prob, dscore = scores_block(query, h, k_block, v_block, first, causal)
                prob_ref[part, column : column + query.rows] = prob
                dscore_ref[part, column : column + query.rows] = dscore
                column += query.rows


def key_terms(queries, part, prob_ref, dscore_ref):
    go = jnp.concatenate([g for query in queries for g in query.go], axis=0)
    q = jnp.concatenate([g for query in queries for g in query.q], axis=0)
    dk = jnp.dot(dscore_ref[part, :], q, preferred_element_type=jnp.float32)
    dv = jnp.dot(prob_ref[part, :], go, preferred_element_type=jnp.float32)
    return jnp.concatenate([dk, dv], axis=1)


def query_terms(kv_ref, dscore_ref):
    e = kv_ref.shape[1] // 2
    return lax.dot_general(
        kv_ref[:, :e], dscore_ref[...], (((0,), (0,)), ((), ())), preferred_element_type=jnp.float32
    )


def place():
    index = lax.axis_index("ctx")
    return index, index // 2, lax.rem(index, 2)


def block_start(chip, back, chips, rows):
    behind = chip - back
    return jnp.where(behind >= 0, behind, -2 * chips) * (2 * rows)


def own_kernel(heads, lens_ref, pay_ref, kv_ref, dqt_ref, keep_ref, give_ref, prob_ref, dscore_ref):
    rows = pay_ref.shape[0] - STAT_ROWS
    e = kv_ref.shape[1] // 2
    index, chip, core = place()
    query = Query(pay_ref, heads, index * rows, lens_ref)
    firsts = [(2 * chip + half) * rows for half in range(2)]
    fill([query], kv_ref, firsts, True, prob_ref, dscore_ref)
    for out_ref, half in ((give_ref, 1 - core), (keep_ref, core)):
        part = pl.ds(pl.multiple_of(half * rows, rows), rows)
        out_ref[...] = key_terms([query], part, prob_ref, dscore_ref)
    dqt = query_terms(kv_ref, dscore_ref)
    for h in range(heads):
        dqt_ref[h * e : (h + 1) * e, :] = dqt[:, h * rows : (h + 1) * rows]


def cross_kernel(
    heads, chips, lens_ref, pay_ref, far_ref, kv_ref, dqt_in_ref, dqt_ref, back_ref, keep_ref, give_ref,
    prob_ref, dscore_ref
):
    rows = pay_ref.shape[0] - STAT_ROWS
    e = kv_ref.shape[1] // 2
    index, chip, core = place()
    own = Query(pay_ref, heads, index * rows, lens_ref)
    far = Query(far_ref, heads, (index + 4) * rows, lens_ref)
    far.start = jnp.where(chip + 2 < chips, far.start, 4 * chips * rows)
    firsts = [
        block_start(chip, b + 1, chips, rows) + half * rows for half in range(2) for b in range(2)
    ]
    fill([own, far], kv_ref, firsts, False, prob_ref, dscore_ref)
    for out_ref, half in ((give_ref, 1 - core), (keep_ref, core)):
        part = pl.ds(pl.multiple_of(half * 2 * rows, rows), 2 * rows)
        out_ref[...] = key_terms([own, far], part, prob_ref, dscore_ref).astype(out_ref.dtype)
    dqt = query_terms(kv_ref, dscore_ref)
    for h in range(heads):
        block = pl.ds(h * e, e)
        dqt_ref[block, :] = dqt_in_ref[block, :] + dqt[:, h * rows : (h + 1) * rows]
        far_part = dqt[:, (heads + h) * rows : (heads + h + 1) * rows]
        back_ref[block, :] = far_part.astype(jnp.bfloat16)


def pair_kernel(keep_ref, both_ref, back_ref, near_ref, far_ref, send_ref):
    send_ref[...] = back_ref[...]
    count = keep_ref.shape[0]
    rows = count // 2
    _, _, core = place()
    other = both_ref[pl.ds(pl.multiple_of((1 - core) * count, count), count), :]
    total = (keep_ref[...] + other.astype(jnp.float32)).astype(jnp.bfloat16)
    near_ref[...] = total[:rows]
    far_ref[...] = total[rows:]


def final_kernel(dqt_ref, keep_ref, both_ref, far_ref, back_ref, near_ref, dq_ref, dk_ref, dv_ref):
    rows = keep_ref.shape[0]
    e = keep_ref.shape[1] // 2
    _, _, core = place()
    dq_ref[...] = (dqt_ref[...] + back_ref[...].astype(jnp.float32)).T.astype(jnp.bfloat16)
    other = both_ref[pl.ds(pl.multiple_of((1 - core) * rows, rows), rows), :]
    total = keep_ref[...] + other
    total = total + near_ref[...].astype(jnp.float32) + far_ref[...].astype(jnp.float32)
    dk_ref[...] = total[:, :e].astype(jnp.bfloat16)
    dv_ref[...] = total[:, e:].astype(jnp.bfloat16)


def call(kernel, outs, name, flops=0, smem=0, space=pltpu.VMEM, scratch=()):
    def run(*args):
        specs = [pl.BlockSpec(memory_space=pltpu.SMEM)] * smem
        specs += [pl.BlockSpec(memory_space=space)] * (len(args) - smem)
        moved = sum(a.size * a.dtype.itemsize for a in args)
        return pl.pallas_call(
            kernel,
            out_shape=[jax.ShapeDtypeStruct(s, d) for s, d in outs],
            in_specs=specs,
            out_specs=[pl.BlockSpec(memory_space=pltpu.VMEM)] * len(outs),
            scratch_shapes=list(scratch),
            cost_estimate=pl.CostEstimate(flops=flops, bytes_accessed=moved, transcendentals=0),
            compiler_params=pltpu.CompilerParams(vmem_limit_bytes=32 * 1024 * 1024),
            name=name,
        )(*args)

    return run


def body(queries, key_states, value_states, attn_out, grad_out, log_norm, doc_lengths):
    rows, width = queries.shape
    heads = log_norm.shape[0]
    e = key_states.shape[1]
    count = lax.axis_size("ctx")
    chips = count // 2
    pairs = [[2 * i, 2 * i + 1] for i in range(chips)]
    bf16, f32 = jnp.bfloat16, jnp.float32

    def shift(x, by):
        return lax.ppermute(x, "ctx", [(i, (i + by) % count) for i in range(count)])

    def pair_gather(x):
        return lax.all_gather(x, "ctx", axis=0, tiled=True, axis_index_groups=pairs)

    pay, kv = call(
        prep_kernel,
        [((rows + STAT_ROWS, 2 * width), bf16), ((rows, 2 * e), bf16)],
        "prep",
        space=pltpu.HBM,
        scratch=[
            pltpu.VMEM((rows, width), bf16),
            pltpu.VMEM((heads, rows), f32),
            pltpu.SemaphoreType.DMA((6,)),
        ],
    )(
        *[
            pltpu.with_memory_space_constraint(x, pltpu.HBM)
            for x in (queries, grad_out, attn_out, log_norm, key_states, value_states)
        ]
    )
    pay_far = shift(pay, -4)
    kv_far = shift(kv, 4)
    kv_near = shift(kv, 2)
    kv_own = pair_gather(kv)
    unit = 5 * 2 * heads * rows * 2 * rows * e
    dqt, keep_own, give_own = call(
        functools.partial(own_kernel, heads),
        [((width, rows), f32), ((rows, 2 * e), f32), ((rows, 2 * e), f32)],
        "own",
        unit,
        1,
        scratch=[pltpu.VMEM((2 * rows, heads * rows), bf16)] * 2,
    )(doc_lengths, pay, kv_own)
    kv_near, kv_far, pay_far = lax.optimization_barrier((kv_near, kv_far, pay_far))
    kv_back = pair_gather(jnp.concatenate([kv_near, kv_far], axis=0))
    dqt, dqt_far, keep, give = call(
        functools.partial(cross_kernel, heads, chips),
        [
            ((width, rows), f32),
            ((width, rows), bf16),
            ((2 * rows, 2 * e), f32),
            ((2 * rows, 2 * e), bf16),
        ],
        "cross",
        4 * unit,
        1,
        scratch=[pltpu.VMEM((4 * rows, 2 * heads * rows), bf16)] * 2,
    )(doc_lengths, pay, pay_far, kv_back, dqt)
    both = pair_gather(give)
    to_near, to_far, to_query = call(
        pair_kernel,
        [((rows, 2 * e), bf16), ((rows, 2 * e), bf16), ((width, rows), bf16)],
        "pair",
    )(keep, both, dqt_far)
    dqt_back = shift(to_query, 4)
    from_far = shift(to_far, -4)
    from_near = shift(to_near, -2)
    both_own = pair_gather(give_own)
    grad_query, grad_key, grad_value = call(
        final_kernel, [((rows, width), bf16), ((rows, e), bf16), ((rows, e), bf16)], "final"
    )(dqt, keep_own, both_own, from_far, dqt_back, from_near)
    return (grad_query, grad_key, grad_value)


def solution(mesh):
    rows = P(("dp", "ctx"), None)
    placed = (rows, rows, rows, rows, rows, P(None, ("dp", "ctx")), P("dp"))
    return jax.shard_map(
        body, mesh=mesh, in_specs=placed, out_specs=(rows, rows, rows), check_vma=False
    )
```

```python
import functools
import math

import jax
import jax.numpy as jnp
from jax import lax
from jax.experimental import pallas as pl
from jax.experimental.pallas import tpu as pltpu
from jax.sharding import PartitionSpec as P

LOG2E = math.log2(math.e)
STAT_ROWS = 16


def split3(value):
    high = value.astype(jnp.bfloat16)
    rest = value - high.astype(jnp.float32)
    mid = rest.astype(jnp.bfloat16)
    low = (rest - mid.astype(jnp.float32)).astype(jnp.bfloat16)
    return high, mid, low


def prep_kernel(q_ref, go_ref, out_ref, norm_ref, k_ref, v_ref, pay_ref, kv_ref, *scratch):
    out_buf, norm_buf, sems = scratch
    rows, width = q_ref.shape
    heads = norm_ref.shape[0]
    e = width // heads
    moves = [
        (go_ref, pay_ref.at[rows : 2 * rows]),
        (out_ref, out_buf),
        (norm_ref, norm_buf),
        (q_ref, pay_ref.at[:rows]),
        (k_ref, kv_ref.at[:, :e]),
        (v_ref, kv_ref.at[:, e:]),
    ]
    copies = [pltpu.make_async_copy(s, d, sems.at[i]) for i, (s, d) in enumerate(moves)]
    for copy in copies:
        copy.start()
    for copy in copies[:3]:
        copy.wait()
    product = pay_ref[rows : 2 * rows].astype(jnp.float32) * out_buf[...].astype(jnp.float32)
    product_t = product.T
    stats = []
    for h in range(heads):
        delta = jnp.sum(product_t[h * e : (h + 1) * e], axis=0, keepdims=True)
        stats += list(split3(norm_buf[h : h + 1, :] * LOG2E)) + list(split3(delta))
    stats += [jnp.zeros((1, rows), jnp.bfloat16)] * (STAT_ROWS - len(stats))
    table = jnp.concatenate([s.astype(jnp.float32) for s in stats], axis=0)
    pay_ref[2 * rows :, :rows] = table.astype(jnp.bfloat16)
    for copy in copies[3:]:
        copy.wait()


class Query:
    def __init__(self, pay_ref, block, heads, first, lens_ref):
        rows, width = (pay_ref.shape[0] // 2 - STAT_ROWS) // 2, pay_ref.shape[1]
        e = width // heads
        base = block * (2 * rows + STAT_ROWS)
        self.heads, self.rows, self.e = heads, rows, e
        self.q = [pay_ref[base : base + rows, h * e : (h + 1) * e] for h in range(heads)]
        self.go = [
            pay_ref[base + rows : base + 2 * rows, h * e : (h + 1) * e] for h in range(heads)
        ]
        table = pay_ref[base + 2 * rows : base + 2 * rows + STAT_ROWS, :rows].astype(jnp.float32)
        row = lambda i: table[i : i + 1]
        self.norm = [row(6 * h) + row(6 * h + 1) + row(6 * h + 2) for h in range(heads)]
        self.delta = [row(6 * h + 3) + row(6 * h + 4) + row(6 * h + 5) for h in range(heads)]
        self.pos = first + lax.broadcasted_iota(jnp.int32, (1, rows), 1)
        self.start = jnp.zeros((1, rows), jnp.int32)
        end = jnp.int32(0)
        for d in range(lens_ref.shape[0]):
            end = end + lens_ref[d]
            self.start = jnp.where(end <= self.pos, end, self.start)


def scores_block(query, h, k_block, v_block, k_first, causal):
    contract = (((1,), (1,)), ((), ()))
    scaling = query.e ** (-0.5)
    scores = lax.dot_general(k_block, query.q[h], contract, preferred_element_type=jnp.float32)
    grads = lax.dot_general(v_block, query.go[h], contract, preferred_element_type=jnp.float32)
    k_pos = k_first + lax.broadcasted_iota(jnp.int32, (k_block.shape[0], 1), 0)
    allowed = k_pos >= query.start
    if causal:
        allowed = allowed & (k_pos <= query.pos)
    prob = jnp.where(allowed, jnp.exp2(scores * (scaling * LOG2E) - query.norm[h]), 0.0)
    dscore = prob * (grads - query.delta[h]) * scaling
    return prob.astype(jnp.bfloat16), dscore.astype(jnp.bfloat16)


def fill(queries, blocks, firsts, causal, prob_ref, dscore_ref):
    for i, (block, first) in enumerate(zip(blocks, firsts)):
        rows, e = block.shape[0], block.shape[1] // 2
        part = pl.ds(i * rows, rows)
        k_block, v_block = block[:, :e], block[:, e:]
        column = 0
        for query in queries:
            for h in range(query.heads):
                prob, dscore = scores_block(query, h, k_block, v_block, first, causal)
                prob_ref[part, column : column + query.rows] = prob
                dscore_ref[part, column : column + query.rows] = dscore
                column += query.rows


def key_terms(queries, part, prob_ref, dscore_ref):
    go = jnp.concatenate([g for query in queries for g in query.go], axis=0)
    q = jnp.concatenate([g for query in queries for g in query.q], axis=0)
    dk = jnp.dot(dscore_ref[part, :], q, preferred_element_type=jnp.float32)
    dv = jnp.dot(prob_ref[part, :], go, preferred_element_type=jnp.float32)
    return jnp.concatenate([dk, dv], axis=1)


def query_terms(keys, dscore):
    return lax.dot_general(
        keys, dscore, (((0,), (0,)), ((), ())), preferred_element_type=jnp.float32
    )


def place():
    index = lax.axis_index("ctx")
    return index, index // 2, lax.rem(index, 2)


def block_start(chip, back, chips, rows):
    behind = chip - back
    return jnp.where(behind >= 0, behind, -2 * chips) * (2 * rows)


def own_kernel(heads, lens_ref, pay_ref, kv_ref, dqt_ref, dkv_ref, prob_ref, dscore_ref):
    rows, e = kv_ref.shape[0], kv_ref.shape[1] // 2
    index, chip, core = place()
    queries = [Query(pay_ref, i, heads, (2 * chip + i) * rows, lens_ref) for i in range(2)]
    fill(queries, [kv_ref[...]], [index * rows], True, prob_ref, dscore_ref)
    dkv_ref[...] = key_terms(queries, pl.ds(0, rows), prob_ref, dscore_ref)
    dqt = query_terms(kv_ref[:, :e], dscore_ref[...])
    for i in range(2):
        for h in range(heads):
            column = (i * heads + h) * rows
            dqt_ref[(i * heads + h) * e : (i * heads + h + 1) * e, :] = dqt[:, column : column + rows]


def cross_kernel(
    heads, chips, lens_ref, own_ref, far_ref, same_ref, other_ref, dqt_in_ref,
    dkv_ref, give_ref, keep_far_ref, keep_own_ref, prob_ref, dscore_ref, dqt_ref
):
    rows, e = same_ref.shape[0], same_ref.shape[1] // 2
    width = heads * e
    index, chip, core = place()
    own = [Query(own_ref, i, heads, (2 * chip + i) * rows, lens_ref) for i in range(2)]
    far = [Query(far_ref, i, heads, (2 * chip + 4 + i) * rows, lens_ref) for i in range(2)]
    for query in far:
        query.start = jnp.where(chip + 2 < chips, query.start, 4 * chips * rows)
    first = block_start(chip, 1 + core, chips, rows)
    firsts = [first + core * rows, first + (1 - core) * rows]
    fill(own + far, [same_ref[...], other_ref[...]], firsts, False, prob_ref, dscore_ref)
    for i, half in enumerate((core, 1 - core)):
        out = pl.ds(pl.multiple_of(half * rows, rows), rows)
        terms = key_terms(own + far, pl.ds(i * rows, rows), prob_ref, dscore_ref)
        dkv_ref[out, :] = terms.astype(jnp.bfloat16)
    dqt = query_terms(same_ref[:, :e], dscore_ref[:rows, :])
    dqt = dqt + query_terms(other_ref[:, :e], dscore_ref[rows:, :])
    for i in range(4 * heads):
        dqt_ref[i * e : (i + 1) * e, :] = dqt[:, i * rows : (i + 1) * rows]
    mine = lambda ref, i: ref[pl.ds(pl.multiple_of(i * width, width), width), :]
    keep_own_ref[...] = mine(dqt_ref, core) + mine(dqt_in_ref, core)
    keep_far_ref[...] = mine(dqt_ref, 2 + core)
    give_ref[:width, :] = mine(dqt_ref, 3 - core).astype(jnp.bfloat16)
    given = mine(dqt_ref, 1 - core) + mine(dqt_in_ref, 1 - core)
    give_ref[width:, :] = given.astype(jnp.bfloat16)


def pair_kernel(keep_ref, both_ref, send_ref):
    width = keep_ref.shape[0]
    _, _, core = place()
    other = both_ref[pl.ds(pl.multiple_of((1 - core) * 2 * width, width), width), :]
    send_ref[...] = (keep_ref[...] + other.astype(jnp.float32)).astype(jnp.bfloat16)


def final_kernel(keep_ref, both_ref, dkv_ref, back_ref, dqt_back_ref, dq_ref, dk_ref, dv_ref):
    width = keep_ref.shape[0]
    rows, e = dkv_ref.shape[0], dkv_ref.shape[1] // 2
    _, _, core = place()
    take = lambda ref, i, size: ref[pl.ds(pl.multiple_of(i * size, size), size), :].astype(jnp.float32)
    dqt = keep_ref[...] + take(both_ref, 2 * (1 - core) + 1, width)
    dq_ref[...] = (dqt + dqt_back_ref[...].astype(jnp.float32)).T.astype(jnp.bfloat16)
    total = dkv_ref[...] + take(back_ref, core, rows) + take(back_ref, 2 + core, rows)
    dk_ref[...] = total[:, :e].astype(jnp.bfloat16)
    dv_ref[...] = total[:, e:].astype(jnp.bfloat16)


def call(kernel, outs, name, flops=0, smem=0, space=pltpu.VMEM, scratch=()):
    def run(*args):
        specs = [pl.BlockSpec(memory_space=pltpu.SMEM)] * smem
        specs += [pl.BlockSpec(memory_space=space)] * (len(args) - smem)
        moved = sum(a.size * a.dtype.itemsize for a in args)
        return pl.pallas_call(
            kernel,
            out_shape=[jax.ShapeDtypeStruct(s, d) for s, d in outs],
            in_specs=specs,
            out_specs=[pl.BlockSpec(memory_space=pltpu.VMEM)] * len(outs),
            scratch_shapes=list(scratch),
            cost_estimate=pl.CostEstimate(flops=flops, bytes_accessed=moved, transcendentals=0),
            compiler_params=pltpu.CompilerParams(vmem_limit_bytes=32 * 1024 * 1024),
            name=name,
        )(*args)

    return run


def body(queries, key_states, value_states, attn_out, grad_out, log_norm, doc_lengths):
    rows, width = queries.shape
    heads = log_norm.shape[0]
    e = key_states.shape[1]
    count = lax.axis_size("ctx")
    chips = count // 2
    pairs = [[2 * i, 2 * i + 1] for i in range(chips)]
    bf16, f32 = jnp.bfloat16, jnp.float32

    def shift(x, by_even, by_odd):
        moves = [(i, i + (by_odd if i % 2 else by_even)) for i in range(count)]
        return lax.ppermute(x, "ctx", [(i, j) for i, j in moves if 0 <= j < count])

    def pair_gather(x):
        return lax.all_gather(x, "ctx", axis=0, tiled=True, axis_index_groups=pairs)

    pay, kv = call(
        prep_kernel,
        [((2 * rows + STAT_ROWS, width), bf16), ((rows, 2 * e), bf16)],
        "prep",
        space=pltpu.HBM,
        scratch=[
            pltpu.VMEM((rows, width), bf16),
            pltpu.VMEM((heads, rows), f32),
            pltpu.SemaphoreType.DMA((6,)),
        ],
    )(
        *[
            pltpu.with_memory_space_constraint(x, pltpu.HBM)
            for x in (queries, grad_out, attn_out, log_norm, key_states, value_states)
        ]
    )
    pay_far = shift(pay, -4, -4)
    kv_same = shift(kv, 2, 4)
    kv_other = shift(kv, 5, 1)
    pay_own = pair_gather(pay)
    unit = 5 * 2 * heads * rows * 2 * rows * e
    dqt, dkv_own = call(
        functools.partial(own_kernel, heads),
        [((2 * width, rows), f32), ((rows, 2 * e), f32)],
        "own",
        unit,
        1,
        scratch=[pltpu.VMEM((rows, 2 * heads * rows), bf16)] * 2,
    )(doc_lengths, pay_own, kv)
    pay_ahead = pair_gather(pay_far)
    dkv, give, keep_far, keep_own = call(
        functools.partial(cross_kernel, heads, chips),
        [((2 * rows, 2 * e), bf16), ((2 * width, rows), bf16), ((width, rows), f32), ((width, rows), f32)],
        "cross",
        4 * unit,
        1,
        scratch=[pltpu.VMEM((2 * rows, 4 * heads * rows), bf16)] * 2
        + [pltpu.VMEM((4 * width, rows), f32)],
    )(doc_lengths, pay_own, pay_ahead, kv_same, kv_other, dqt)
    dkv_back = shift(dkv, -2, -4)
    both = pair_gather(give)
    (to_query,) = call(pair_kernel, [((width, rows), bf16)], "pair")(keep_far, both)
    dqt_back = shift(to_query, 4, 4)
    back = pair_gather(dkv_back)
    grad_query, grad_key, grad_value = call(
        final_kernel, [((rows, width), bf16), ((rows, e), bf16), ((rows, e), bf16)], "final"
    )(keep_own, both, dkv_own, back, dqt_back)
    return (grad_query, grad_key, grad_value)


def solution(mesh):
    rows = P(("dp", "ctx"), None)
    placed = (rows, rows, rows, rows, rows, P(None, ("dp", "ctx")), P("dp"))
    return jax.shard_map(
        body, mesh=mesh, in_specs=placed, out_specs=(rows, rows, rows), check_vma=False
    )
```

```python
import functools
import math

import jax
import jax.numpy as jnp
from jax import lax
from jax.experimental import pallas as pl
from jax.experimental.pallas import tpu as pltpu
from jax.sharding import PartitionSpec as P

LOG2E = math.log2(math.e)
STAT_ROWS = 16


def split3(value):
    high = value.astype(jnp.bfloat16)
    rest = value - high.astype(jnp.float32)
    mid = rest.astype(jnp.bfloat16)
    low = (rest - mid.astype(jnp.float32)).astype(jnp.bfloat16)
    return high, mid, low


def prep_kernel(q_ref, go_ref, out_ref, norm_ref, k_ref, v_ref, pay_ref, kv_ref, *scratch):
    out_buf, norm_buf, sems = scratch
    rows, width = q_ref.shape
    heads = norm_ref.shape[0]
    e = width // heads
    moves = [
        (go_ref, pay_ref.at[rows : 2 * rows]),
        (out_ref, out_buf),
        (norm_ref, norm_buf),
        (q_ref, pay_ref.at[:rows]),
        (k_ref, kv_ref.at[:, :e]),
        (v_ref, kv_ref.at[:, e:]),
    ]
    copies = [pltpu.make_async_copy(s, d, sems.at[i]) for i, (s, d) in enumerate(moves)]
    for copy in copies:
        copy.start()
    for copy in copies[:3]:
        copy.wait()
    product = pay_ref[rows : 2 * rows].astype(jnp.float32) * out_buf[...].astype(jnp.float32)
    product_t = product.T
    stats = []
    for h in range(heads):
        delta = jnp.sum(product_t[h * e : (h + 1) * e], axis=0, keepdims=True)
        stats += list(split3(norm_buf[h : h + 1, :] * LOG2E)) + list(split3(delta))
    stats += [jnp.zeros((1, rows), jnp.bfloat16)] * (STAT_ROWS - len(stats))
    table = jnp.concatenate([s.astype(jnp.float32) for s in stats], axis=0)
    pay_ref[2 * rows :, :rows] = table.astype(jnp.bfloat16)
    for copy in copies[3:]:
        copy.wait()


class Query:
    def __init__(self, pay_ref, block, heads, first, lens_ref):
        rows, width = (pay_ref.shape[0] // 2 - STAT_ROWS) // 2, pay_ref.shape[1]
        e = width // heads
        base = block * (2 * rows + STAT_ROWS)
        self.heads, self.rows, self.e = heads, rows, e
        self.q = [pay_ref[base : base + rows, h * e : (h + 1) * e] for h in range(heads)]
        self.go = [
            pay_ref[base + rows : base + 2 * rows, h * e : (h + 1) * e] for h in range(heads)
        ]
        table = pay_ref[base + 2 * rows : base + 2 * rows + STAT_ROWS, :rows].astype(jnp.float32)
        row = lambda i: table[i : i + 1]
        self.norm = [row(6 * h) + row(6 * h + 1) + row(6 * h + 2) for h in range(heads)]
        self.delta = [row(6 * h + 3) + row(6 * h + 4) + row(6 * h + 5) for h in range(heads)]
        self.pos = first + lax.broadcasted_iota(jnp.int32, (1, rows), 1)
        self.start = jnp.zeros((1, rows), jnp.int32)
        end = jnp.int32(0)
        for d in range(lens_ref.shape[0]):
            end = end + lens_ref[d]
            self.start = jnp.where(end <= self.pos, end, self.start)


def scores_block(query, h, k_block, v_block, k_first, causal):
    contract = (((1,), (1,)), ((), ()))
    scaling = query.e ** (-0.5)
    scores = lax.dot_general(k_block, query.q[h], contract, preferred_element_type=jnp.float32)
    grads = lax.dot_general(v_block, query.go[h], contract, preferred_element_type=jnp.float32)
    k_pos = k_first + lax.broadcasted_iota(jnp.int32, (k_block.shape[0], 1), 0)
    allowed = k_pos >= query.start
    if causal:
        allowed = allowed & (k_pos <= query.pos)
    prob = jnp.where(allowed, jnp.exp2(scores * (scaling * LOG2E) - query.norm[h]), 0.0)
    dscore = prob * (grads - query.delta[h]) * scaling
    return prob.astype(jnp.bfloat16), dscore.astype(jnp.bfloat16)


def fill(queries, blocks, firsts, causal, prob_ref, dscore_ref):
    for i, (block, first) in enumerate(zip(blocks, firsts)):
        rows, e = block.shape[0], block.shape[1] // 2
        part = pl.ds(i * rows, rows)
        k_block, v_block = block[:, :e], block[:, e:]
        column = 0
        for query in queries:
            for h in range(query.heads):
                prob, dscore = scores_block(query, h, k_block, v_block, first, causal)
                prob_ref[part, column : column + query.rows] = prob
                dscore_ref[part, column : column + query.rows] = dscore
                column += query.rows


def key_terms(queries, part, prob_ref, dscore_ref):
    go = jnp.concatenate([g for query in queries for g in query.go], axis=0)
    q = jnp.concatenate([g for query in queries for g in query.q], axis=0)
    dk = jnp.dot(dscore_ref[part, :], q, preferred_element_type=jnp.float32)
    dv = jnp.dot(prob_ref[part, :], go, preferred_element_type=jnp.float32)
    return jnp.concatenate([dk, dv], axis=1)


def query_terms(keys, dscore):
    return lax.dot_general(
        keys, dscore, (((0,), (0,)), ((), ())), preferred_element_type=jnp.float32
    )


def place():
    index = lax.axis_index("ctx")
    return index, index // 2, lax.rem(index, 2)


def block_start(chip, back, chips, rows):
    behind = chip - back
    return jnp.where(behind >= 0, behind, -2 * chips) * (2 * rows)


def own_kernel(heads, lens_ref, pay_ref, kv_ref, dqt_ref, dkv_ref, prob_ref, dscore_ref):
    rows, e = kv_ref.shape[0], kv_ref.shape[1] // 2
    index, chip, core = place()
    queries = [Query(pay_ref, i, heads, (2 * chip + i) * rows, lens_ref) for i in range(2)]
    fill(queries, [kv_ref[...]], [index * rows], True, prob_ref, dscore_ref)
    dkv_ref[...] = key_terms(queries, pl.ds(0, rows), prob_ref, dscore_ref)
    dqt = query_terms(kv_ref[:, :e], dscore_ref[...])
    for i in range(2):
        for h in range(heads):
            column = (i * heads + h) * rows
            dqt_ref[(i * heads + h) * e : (i * heads + h + 1) * e, :] = dqt[:, column : column + rows]


def near_kernel(
    heads, chips, lens_ref, own_ref, same_ref, dqt_in_ref, dqt_ref, dkv_ref, prob_ref, dscore_ref
):
    rows, e = same_ref.shape[0], same_ref.shape[1] // 2
    index, chip, core = place()
    own = [Query(own_ref, i, heads, (2 * chip + i) * rows, lens_ref) for i in range(2)]
    first = block_start(chip, 1 + core, chips, rows) + core * rows
    fill(own, [same_ref[...]], [first], False, prob_ref, dscore_ref)
    dkv_ref[...] = key_terms(own, pl.ds(0, rows), prob_ref, dscore_ref)
    dqt = query_terms(same_ref[:, :e], dscore_ref[...])
    for i in range(2 * heads):
        block = pl.ds(i * e, e)
        dqt_ref[block, :] = dqt_in_ref[block, :] + dqt[:, i * rows : (i + 1) * rows]


def cross_kernel(
    heads, chips, lens_ref, own_ref, far_ref, same_ref, other_ref, dqt_in_ref, dkv_in_ref,
    dkv_ref, give_ref, keep_far_ref, keep_own_ref, prob_ref, dscore_ref, dqt_ref
):
    rows, e = same_ref.shape[0], same_ref.shape[1] // 2
    width = heads * e
    index, chip, core = place()
    own = [Query(own_ref, i, heads, (2 * chip + i) * rows, lens_ref) for i in range(2)]
    far = [Query(far_ref, i, heads, (2 * chip + 4 + i) * rows, lens_ref) for i in range(2)]
    for query in far:
        query.start = jnp.where(chip + 2 < chips, query.start, 4 * chips * rows)
    first = block_start(chip, 1 + core, chips, rows)
    half = 2 * heads * rows
    probs = [prob_ref.at[:rows, half:], prob_ref.at[rows:, :]]
    dscores = [dscore_ref.at[:rows, half:], dscore_ref.at[rows:, :]]
    fill(far, [same_ref[...]], [first + core * rows], False, probs[0], dscores[0])
    fill(own + far, [other_ref[...]], [first + (1 - core) * rows], False, probs[1], dscores[1])
    same = dkv_in_ref[...] + key_terms(far, pl.ds(0, rows), probs[0], dscores[0])
    other = key_terms(own + far, pl.ds(0, rows), probs[1], dscores[1])
    dkv_ref[pl.ds(pl.multiple_of(core * rows, rows), rows), :] = same.astype(jnp.bfloat16)
    dkv_ref[pl.ds(pl.multiple_of((1 - core) * rows, rows), rows), :] = other.astype(jnp.bfloat16)
    dqt = query_terms(other_ref[:, :e], dscores[1][...])
    dqt_far = query_terms(same_ref[:, :e], dscores[0][...])
    for i in range(2 * heads):
        block = pl.ds(i * e, e)
        columns = slice(i * rows, (i + 1) * rows)
        dqt_ref[block, :] = dqt_in_ref[block, :] + dqt[:, columns]
        dqt_ref[pl.ds(2 * width + i * e, e), :] = dqt[:, half:][:, columns] + dqt_far[:, columns]
    mine = lambda i: dqt_ref[pl.ds(pl.multiple_of(i * width, width), width), :]
    keep_own_ref[...] = mine(core)
    keep_far_ref[...] = mine(2 + core)
    give_ref[:width, :] = mine(3 - core).astype(jnp.bfloat16)
    give_ref[width:, :] = mine(1 - core).astype(jnp.bfloat16)


def pair_kernel(keep_ref, both_ref, send_ref):
    width = keep_ref.shape[0]
    _, _, core = place()
    other = both_ref[pl.ds(pl.multiple_of((1 - core) * 2 * width, width), width), :]
    send_ref[...] = (keep_ref[...] + other.astype(jnp.float32)).astype(jnp.bfloat16)


def final_kernel(keep_ref, both_ref, dkv_ref, back_ref, dqt_back_ref, dq_ref, dk_ref, dv_ref):
    width = keep_ref.shape[0]
    rows, e = dkv_ref.shape[0], dkv_ref.shape[1] // 2
    _, _, core = place()
    take = lambda ref, i, size: ref[pl.ds(pl.multiple_of(i * size, size), size), :].astype(jnp.float32)
    dqt = keep_ref[...] + take(both_ref, 2 * (1 - core) + 1, width)
    dq_ref[...] = (dqt + dqt_back_ref[...].astype(jnp.float32)).T.astype(jnp.bfloat16)
    total = dkv_ref[...] + take(back_ref, core, rows) + take(back_ref, 2 + core, rows)
    dk_ref[...] = total[:, :e].astype(jnp.bfloat16)
    dv_ref[...] = total[:, e:].astype(jnp.bfloat16)


def call(kernel, outs, name, flops=0, smem=0, space=pltpu.VMEM, scratch=()):
    def run(*args):
        specs = [pl.BlockSpec(memory_space=pltpu.SMEM)] * smem
        specs += [pl.BlockSpec(memory_space=space)] * (len(args) - smem)
        moved = sum(a.size * a.dtype.itemsize for a in args)
        return pl.pallas_call(
            kernel,
            out_shape=[jax.ShapeDtypeStruct(s, d) for s, d in outs],
            in_specs=specs,
            out_specs=[pl.BlockSpec(memory_space=pltpu.VMEM)] * len(outs),
            scratch_shapes=list(scratch),
            cost_estimate=pl.CostEstimate(flops=flops, bytes_accessed=moved, transcendentals=0),
            compiler_params=pltpu.CompilerParams(vmem_limit_bytes=32 * 1024 * 1024),
            name=name,
        )(*args)

    return run


def body(queries, key_states, value_states, attn_out, grad_out, log_norm, doc_lengths):
    rows, width = queries.shape
    heads = log_norm.shape[0]
    e = key_states.shape[1]
    count = lax.axis_size("ctx")
    chips = count // 2
    pairs = [[2 * i, 2 * i + 1] for i in range(chips)]
    bf16, f32 = jnp.bfloat16, jnp.float32

    def shift(x, by_even, by_odd, least=0):
        moves = [(i, i + (by_odd if i % 2 else by_even)) for i in range(count)]
        return lax.ppermute(x, "ctx", [(i, j) for i, j in moves if least <= i and least <= j < count])

    def pair_gather(x):
        return lax.all_gather(x, "ctx", axis=0, tiled=True, axis_index_groups=pairs)

    pay, kv = call(
        prep_kernel,
        [((2 * rows + STAT_ROWS, width), bf16), ((rows, 2 * e), bf16)],
        "prep",
        space=pltpu.HBM,
        scratch=[
            pltpu.VMEM((rows, width), bf16),
            pltpu.VMEM((heads, rows), f32),
            pltpu.SemaphoreType.DMA((6,)),
        ],
    )(
        *[
            pltpu.with_memory_space_constraint(x, pltpu.HBM)
            for x in (queries, grad_out, attn_out, log_norm, key_states, value_states)
        ]
    )
    pay_far = shift(pay, -4, -4, 2)
    kv_same = shift(kv, 2, 4)
    kv_other = shift(kv, 5, 1)
    pay_own = pair_gather(pay)
    unit = 5 * 2 * heads * rows * 2 * rows * e
    dqt, dkv_own = call(
        functools.partial(own_kernel, heads),
        [((2 * width, rows), f32), ((rows, 2 * e), f32)],
        "own",
        unit,
        1,
        scratch=[pltpu.VMEM((rows, 2 * heads * rows), bf16)] * 2,
    )(doc_lengths, pay_own, kv)
    dqt, dkv_same = call(
        functools.partial(near_kernel, heads, chips),
        [((2 * width, rows), f32), ((rows, 2 * e), f32)],
        "near",
        unit,
        1,
        scratch=[pltpu.VMEM((rows, 2 * heads * rows), bf16)] * 2,
    )(doc_lengths, pay_own, kv_same, dqt)
    pay_far, kv_other = lax.optimization_barrier((pay_far, kv_other))
    pay_ahead = pair_gather(pay_far)
    dkv, give, keep_far, keep_own = call(
        functools.partial(cross_kernel, heads, chips),
        [((2 * rows, 2 * e), bf16), ((2 * width, rows), bf16), ((width, rows), f32), ((width, rows), f32)],
        "cross",
        3 * unit,
        1,
        scratch=[pltpu.VMEM((2 * rows, 4 * heads * rows), bf16)] * 2
        + [pltpu.VMEM((4 * width, rows), f32)],
    )(doc_lengths, pay_own, pay_ahead, kv_same, kv_other, dqt, dkv_same)
    dkv_back = shift(dkv, -2, -4)
    both = pair_gather(give)
    (to_query,) = call(pair_kernel, [((width, rows), bf16)], "pair")(keep_far, both)
    dqt_back = shift(to_query, 4, 4, 2)
    back = pair_gather(dkv_back)
    grad_query, grad_key, grad_value = call(
        final_kernel, [((rows, width), bf16), ((rows, e), bf16), ((rows, e), bf16)], "final"
    )(keep_own, both, dkv_own, back, dqt_back)
    return (grad_query, grad_key, grad_value)


def solution(mesh):
    rows = P(("dp", "ctx"), None)
    placed = (rows, rows, rows, rows, rows, P(None, ("dp", "ctx")), P("dp"))
    return jax.shard_map(
        body, mesh=mesh, in_specs=placed, out_specs=(rows, rows, rows), check_vma=False
    )
```

```python
import functools
import math

import jax
import jax.numpy as jnp
from jax import lax
from jax.experimental import pallas as pl
from jax.experimental.pallas import tpu as pltpu
from jax.sharding import PartitionSpec as P

LOG2E = math.log2(math.e)
STAT_ROWS = 16


def split3(value):
    high = value.astype(jnp.bfloat16)
    rest = value - high.astype(jnp.float32)
    mid = rest.astype(jnp.bfloat16)
    low = (rest - mid.astype(jnp.float32)).astype(jnp.bfloat16)
    return high, mid, low


def prep_kernel(q_ref, go_ref, out_ref, norm_ref, k_ref, v_ref, pay_ref, kv_ref, *scratch):
    out_buf, norm_buf, sems = scratch
    rows, width = q_ref.shape
    heads = norm_ref.shape[0]
    e = width // heads
    moves = [
        (go_ref, pay_ref.at[rows : 2 * rows]),
        (out_ref, out_buf),
        (norm_ref, norm_buf),
        (q_ref, pay_ref.at[:rows]),
        (k_ref, kv_ref.at[:, :e]),
        (v_ref, kv_ref.at[:, e:]),
    ]
    copies = [pltpu.make_async_copy(s, d, sems.at[i]) for i, (s, d) in enumerate(moves)]
    for copy in copies:
        copy.start()
    for copy in copies[:3]:
        copy.wait()
    product = pay_ref[rows : 2 * rows].astype(jnp.float32) * out_buf[...].astype(jnp.float32)
    product_t = product.T
    stats = []
    for h in range(heads):
        delta = jnp.sum(product_t[h * e : (h + 1) * e], axis=0, keepdims=True)
        stats += list(split3(norm_buf[h : h + 1, :] * LOG2E)) + list(split3(delta))
    stats += [jnp.zeros((1, rows), jnp.bfloat16)] * (STAT_ROWS - len(stats))
    table = jnp.concatenate([s.astype(jnp.float32) for s in stats], axis=0)
    pay_ref[2 * rows :, :rows] = table.astype(jnp.bfloat16)
    for copy in copies[3:]:
        copy.wait()


class Query:
    def __init__(self, pay_ref, block, heads, first, lens_ref):
        rows, width = (pay_ref.shape[0] // 2 - STAT_ROWS) // 2, pay_ref.shape[1]
        e = width // heads
        base = block * (2 * rows + STAT_ROWS)
        self.heads, self.rows, self.e = heads, rows, e
        part = lambda at, size: pl.ds(pl.multiple_of(base + at, STAT_ROWS), size)
        self.q = [pay_ref[part(0, rows), h * e : (h + 1) * e] for h in range(heads)]
        self.go = [pay_ref[part(rows, rows), h * e : (h + 1) * e] for h in range(heads)]
        table = pay_ref[part(2 * rows, STAT_ROWS), :rows].astype(jnp.float32)
        row = lambda i: table[i : i + 1]
        self.norm = [row(6 * h) + row(6 * h + 1) + row(6 * h + 2) for h in range(heads)]
        self.delta = [row(6 * h + 3) + row(6 * h + 4) + row(6 * h + 5) for h in range(heads)]
        self.pos = first + lax.broadcasted_iota(jnp.int32, (1, rows), 1)
        self.start = jnp.zeros((1, rows), jnp.int32)
        end = jnp.int32(0)
        for d in range(lens_ref.shape[0]):
            end = end + lens_ref[d]
            self.start = jnp.where(end <= self.pos, end, self.start)


def scores_block(query, h, k_block, v_block, k_first, causal):
    contract = (((1,), (1,)), ((), ()))
    scaling = query.e ** (-0.5)
    scores = lax.dot_general(k_block, query.q[h], contract, preferred_element_type=jnp.float32)
    grads = lax.dot_general(v_block, query.go[h], contract, preferred_element_type=jnp.float32)
    k_pos = k_first + lax.broadcasted_iota(jnp.int32, (k_block.shape[0], 1), 0)
    allowed = k_pos >= query.start
    if causal:
        allowed = allowed & (k_pos <= query.pos)
    prob = jnp.where(allowed, jnp.exp2(scores * (scaling * LOG2E) - query.norm[h]), 0.0)
    dscore = prob * (grads - query.delta[h]) * scaling
    return prob.astype(jnp.bfloat16), dscore.astype(jnp.bfloat16)


def fill(queries, blocks, firsts, causal, prob_ref, dscore_ref):
    for i, (block, first) in enumerate(zip(blocks, firsts)):
        rows, e = block.shape[0], block.shape[1] // 2
        part = pl.ds(i * rows, rows)
        k_block, v_block = block[:, :e], block[:, e:]
        column = 0
        for query in queries:
            for h in range(query.heads):
                prob, dscore = scores_block(query, h, k_block, v_block, first, causal)
                prob_ref[part, column : column + query.rows] = prob
                dscore_ref[part, column : column + query.rows] = dscore
                column += query.rows


def key_terms(queries, part, prob_ref, dscore_ref):
    go = jnp.concatenate([g for query in queries for g in query.go], axis=0)
    q = jnp.concatenate([g for query in queries for g in query.q], axis=0)
    dk = jnp.dot(dscore_ref[part, :], q, preferred_element_type=jnp.float32)
    dv = jnp.dot(prob_ref[part, :], go, preferred_element_type=jnp.float32)
    return jnp.concatenate([dk, dv], axis=1)


def query_terms(keys, dscore):
    return lax.dot_general(
        keys, dscore, (((0,), (0,)), ((), ())), preferred_element_type=jnp.float32
    )


def place():
    index = lax.axis_index("ctx")
    return index, index // 2, lax.rem(index, 2)


def block_start(chip, back, chips, rows):
    behind = chip - back
    return jnp.where(behind >= 0, behind, -2 * chips) * (2 * rows)


def both_halves(pay_ref, heads, chip, core, rows, lens_ref):
    return [
        Query(pay_ref, half, heads, (2 * chip + half) * rows, lens_ref) for half in (core, 1 - core)
    ]


def own_kernel(heads, lens_ref, pay_ref, kv_ref, dqt_ref, dkv_ref, prob_ref, dscore_ref):
    rows, e = kv_ref.shape[0], kv_ref.shape[1] // 2
    index, chip, core = place()
    queries = both_halves(pay_ref, heads, chip, core, rows, lens_ref)
    fill(queries, [kv_ref[...]], [index * rows], True, prob_ref, dscore_ref)
    dkv_ref[...] = key_terms(queries, pl.ds(0, rows), prob_ref, dscore_ref)
    dqt = query_terms(kv_ref[:, :e], dscore_ref[...])
    for i in range(2):
        for h in range(heads):
            column = (i * heads + h) * rows
            dqt_ref[(i * heads + h) * e : (i * heads + h + 1) * e, :] = dqt[:, column : column + rows]


def near_kernel(
    heads, chips, lens_ref, own_ref, same_ref, dqt_in_ref, dqt_ref, dkv_ref, prob_ref, dscore_ref
):
    rows, e = same_ref.shape[0], same_ref.shape[1] // 2
    index, chip, core = place()
    own = both_halves(own_ref, heads, chip, core, rows, lens_ref)
    first = block_start(chip, 1 + core, chips, rows) + core * rows
    fill(own, [same_ref[...]], [first], False, prob_ref, dscore_ref)
    dkv_ref[...] = key_terms(own, pl.ds(0, rows), prob_ref, dscore_ref)
    dqt = query_terms(same_ref[:, :e], dscore_ref[...])
    for i in range(2 * heads):
        block = pl.ds(i * e, e)
        dqt_ref[block, :] = dqt_in_ref[block, :] + dqt[:, i * rows : (i + 1) * rows]


def cross_kernel(
    heads, chips, lens_ref, own_ref, far_ref, same_ref, other_ref, dqt_in_ref, dkv_in_ref,
    dkv_ref, give_ref, keep_far_ref, keep_own_ref, prob_ref, dscore_ref
):
    rows, e = same_ref.shape[0], same_ref.shape[1] // 2
    index, chip, core = place()
    own = both_halves(own_ref, heads, chip, core, rows, lens_ref)
    far = both_halves(far_ref, heads, chip + 2, core, rows, lens_ref)
    for query in far:
        query.start = jnp.where(chip + 2 < chips, query.start, 4 * chips * rows)
    first = block_start(chip, 1 + core, chips, rows)
    half = 2 * heads * rows
    far_prob, far_dscore = prob_ref.at[:, half:], dscore_ref.at[:, half:]
    own_prob, own_dscore = prob_ref.at[rows:, :half], dscore_ref.at[rows:, :half]
    firsts = [first + core * rows, first + (1 - core) * rows]
    fill(far, [same_ref[...], other_ref[...]], firsts, False, far_prob, far_dscore)
    fill(own, [other_ref[...]], firsts[1:], False, own_prob, own_dscore)
    terms = key_terms(far, pl.ds(0, 2 * rows), far_prob, far_dscore)
    same = terms[:rows] + dkv_in_ref[...]
    other = terms[rows:] + key_terms(own, pl.ds(0, rows), own_prob, own_dscore)
    dkv_ref[pl.ds(pl.multiple_of(core * rows, rows), rows), :] = same.astype(jnp.bfloat16)
    dkv_ref[pl.ds(pl.multiple_of((1 - core) * rows, rows), rows), :] = other.astype(jnp.bfloat16)
    keys = jnp.concatenate([same_ref[:, :e], other_ref[:, :e]], axis=0)
    dqt = query_terms(other_ref[:, :e], own_dscore[...])
    dqt_far = query_terms(keys, far_dscore[...])
    for i in range(2 * heads):
        columns = slice(i * rows, (i + 1) * rows)
        own_part = dqt_in_ref[i * e : (i + 1) * e, :] + dqt[:, columns]
        far_part = dqt_far[:, columns]
        if i < heads:
            block = pl.ds(i * e, e)
            keep_own_ref[block, :] = own_part
            keep_far_ref[block, :] = far_part
        else:
            give_ref[pl.ds((i - heads) * e, e), :] = far_part.astype(jnp.bfloat16)
            give_ref[pl.ds(i * e, e), :] = own_part.astype(jnp.bfloat16)


def pair_kernel(keep_ref, both_ref, send_ref):
    width = keep_ref.shape[0]
    _, _, core = place()
    other = both_ref[pl.ds(pl.multiple_of((1 - core) * 2 * width, width), width), :]
    send_ref[...] = (keep_ref[...] + other.astype(jnp.float32)).astype(jnp.bfloat16)


def final_kernel(keep_ref, both_ref, dkv_ref, back_ref, dqt_back_ref, dq_ref, dk_ref, dv_ref):
    width = keep_ref.shape[0]
    rows, e = dkv_ref.shape[0], dkv_ref.shape[1] // 2
    _, _, core = place()
    take = lambda ref, i, size: ref[pl.ds(pl.multiple_of(i * size, size), size), :].astype(jnp.float32)
    dqt = keep_ref[...] + take(both_ref, 2 * (1 - core) + 1, width)
    dq_ref[...] = (dqt + dqt_back_ref[...].astype(jnp.float32)).T.astype(jnp.bfloat16)
    total = dkv_ref[...] + take(back_ref, core, rows) + take(back_ref, 2 + core, rows)
    dk_ref[...] = total[:, :e].astype(jnp.bfloat16)
    dv_ref[...] = total[:, e:].astype(jnp.bfloat16)


def call(kernel, outs, name, flops=0, smem=0, space=pltpu.VMEM, scratch=()):
    def run(*args):
        specs = [pl.BlockSpec(memory_space=pltpu.SMEM)] * smem
        specs += [pl.BlockSpec(memory_space=space)] * (len(args) - smem)
        moved = sum(a.size * a.dtype.itemsize for a in args)
        return pl.pallas_call(
            kernel,
            out_shape=[jax.ShapeDtypeStruct(s, d) for s, d in outs],
            in_specs=specs,
            out_specs=[pl.BlockSpec(memory_space=pltpu.VMEM)] * len(outs),
            scratch_shapes=list(scratch),
            cost_estimate=pl.CostEstimate(flops=flops, bytes_accessed=moved, transcendentals=0),
            compiler_params=pltpu.CompilerParams(vmem_limit_bytes=32 * 1024 * 1024),
            name=name,
        )(*args)

    return run


def body(queries, key_states, value_states, attn_out, grad_out, log_norm, doc_lengths):
    rows, width = queries.shape
    heads = log_norm.shape[0]
    e = key_states.shape[1]
    count = lax.axis_size("ctx")
    chips = count // 2
    pairs = [[2 * i, 2 * i + 1] for i in range(chips)]
    bf16, f32 = jnp.bfloat16, jnp.float32

    def shift(x, by_even, by_odd, least=0):
        moves = [(i, i + (by_odd if i % 2 else by_even)) for i in range(count)]
        return lax.ppermute(x, "ctx", [(i, j) for i, j in moves if least <= i and least <= j < count])

    def pair_gather(x):
        return lax.all_gather(x, "ctx", axis=0, tiled=True, axis_index_groups=pairs)

    pay, kv = call(
        prep_kernel,
        [((2 * rows + STAT_ROWS, width), bf16), ((rows, 2 * e), bf16)],
        "prep",
        space=pltpu.HBM,
        scratch=[
            pltpu.VMEM((rows, width), bf16),
            pltpu.VMEM((heads, rows), f32),
            pltpu.SemaphoreType.DMA((6,)),
        ],
    )(
        *[
            pltpu.with_memory_space_constraint(x, pltpu.HBM)
            for x in (queries, grad_out, attn_out, log_norm, key_states, value_states)
        ]
    )
    pay_far = shift(pay, -4, -4, 2)
    kv_same = shift(kv, 2, 4)
    kv_other = shift(kv, 5, 1)
    pay_own = pair_gather(pay)
    unit = 5 * 2 * heads * rows * 2 * rows * e
    dqt, dkv_own = call(
        functools.partial(own_kernel, heads),
        [((2 * width, rows), f32), ((rows, 2 * e), f32)],
        "own",
        unit,
        1,
        scratch=[pltpu.VMEM((rows, 2 * heads * rows), bf16)] * 2,
    )(doc_lengths, pay_own, kv)
    dqt, dkv_same = call(
        functools.partial(near_kernel, heads, chips),
        [((2 * width, rows), f32), ((rows, 2 * e), f32)],
        "near",
        unit,
        1,
        scratch=[pltpu.VMEM((rows, 2 * heads * rows), bf16)] * 2,
    )(doc_lengths, pay_own, kv_same, dqt)
    pay_far, kv_other = lax.optimization_barrier((pay_far, kv_other))
    pay_ahead = pair_gather(pay_far)
    dkv, give, keep_far, keep_own = call(
        functools.partial(cross_kernel, heads, chips),
        [((2 * rows, 2 * e), bf16), ((2 * width, rows), bf16), ((width, rows), f32), ((width, rows), f32)],
        "cross",
        3 * unit,
        1,
        scratch=[pltpu.VMEM((2 * rows, 4 * heads * rows), bf16)] * 2,
    )(doc_lengths, pay_own, pay_ahead, kv_same, kv_other, dqt, dkv_same)
    dkv_back = shift(dkv, -2, -4)
    both = pair_gather(give)
    (to_query,) = call(pair_kernel, [((width, rows), bf16)], "pair")(keep_far, both)
    dqt_back = shift(to_query, 4, 4, 2)
    back = pair_gather(dkv_back)
    grad_query, grad_key, grad_value = call(
        final_kernel, [((rows, width), bf16), ((rows, e), bf16), ((rows, e), bf16)], "final"
    )(keep_own, both, dkv_own, back, dqt_back)
    return (grad_query, grad_key, grad_value)


def solution(mesh):
    rows = P(("dp", "ctx"), None)
    placed = (rows, rows, rows, rows, rows, P(None, ("dp", "ctx")), P("dp"))
    return jax.shard_map(
        body, mesh=mesh, in_specs=placed, out_specs=(rows, rows, rows), check_vma=False
    )
```

```python
import functools
import math

import jax
import jax.numpy as jnp
from jax import lax
from jax.experimental import pallas as pl
from jax.experimental.pallas import tpu as pltpu
from jax.sharding import PartitionSpec as P

LOG2E = math.log2(math.e)
STAT_ROWS = 16


def split3(value):
    high = value.astype(jnp.bfloat16)
    rest = value - high.astype(jnp.float32)
    mid = rest.astype(jnp.bfloat16)
    low = (rest - mid.astype(jnp.float32)).astype(jnp.bfloat16)
    return high, mid, low


def prep_kernel(q_ref, go_ref, out_ref, norm_ref, k_ref, v_ref, pay_ref, kv_ref, *scratch):
    out_buf, norm_buf, sems = scratch
    rows, width = q_ref.shape
    heads = norm_ref.shape[0]
    e = width // heads
    moves = [
        (go_ref, pay_ref.at[rows : 2 * rows]),
        (out_ref, out_buf),
        (norm_ref, norm_buf),
        (q_ref, pay_ref.at[:rows]),
        (k_ref, kv_ref.at[:, :e]),
        (v_ref, kv_ref.at[:, e:]),
    ]
    copies = [pltpu.make_async_copy(s, d, sems.at[i]) for i, (s, d) in enumerate(moves)]
    for copy in copies:
        copy.start()
    for copy in copies[:3]:
        copy.wait()
    product = pay_ref[rows : 2 * rows].astype(jnp.float32) * out_buf[...].astype(jnp.float32)
    product_t = product.T
    stats = []
    for h in range(heads):
        delta = jnp.sum(product_t[h * e : (h + 1) * e], axis=0, keepdims=True)
        stats += list(split3(norm_buf[h : h + 1, :] * LOG2E)) + list(split3(delta))
    stats += [jnp.zeros((1, rows), jnp.bfloat16)] * (STAT_ROWS - len(stats))
    table = jnp.concatenate([s.astype(jnp.float32) for s in stats], axis=0)
    pay_ref[2 * rows :, :rows] = table.astype(jnp.bfloat16)
    for copy in copies[3:]:
        copy.wait()


class Query:
    def __init__(self, pay_ref, block, heads, first, lens_ref):
        rows, width = (pay_ref.shape[0] // 2 - STAT_ROWS) // 2, pay_ref.shape[1]
        e = width // heads
        base = block * (2 * rows + STAT_ROWS)
        self.heads, self.rows, self.e = heads, rows, e
        part = lambda at, size: pl.ds(pl.multiple_of(base + at, STAT_ROWS), size)
        self.q = [pay_ref[part(0, rows), h * e : (h + 1) * e] for h in range(heads)]
        self.go = [pay_ref[part(rows, rows), h * e : (h + 1) * e] for h in range(heads)]
        table = pay_ref[part(2 * rows, STAT_ROWS), :rows].astype(jnp.float32)
        row = lambda i: table[i : i + 1]
        self.norm = [row(6 * h) + row(6 * h + 1) + row(6 * h + 2) for h in range(heads)]
        self.delta = [row(6 * h + 3) + row(6 * h + 4) + row(6 * h + 5) for h in range(heads)]
        self.pos = first + lax.broadcasted_iota(jnp.int32, (1, rows), 1)
        self.start = jnp.zeros((1, rows), jnp.int32)
        end = jnp.int32(0)
        for d in range(lens_ref.shape[0]):
            end = end + lens_ref[d]
            self.start = jnp.where(end <= self.pos, end, self.start)


def scores_block(query, h, k_block, v_block, k_first, causal):
    contract = (((1,), (1,)), ((), ()))
    scaling = query.e ** (-0.5)
    scores = lax.dot_general(k_block, query.q[h], contract, preferred_element_type=jnp.float32)
    grads = lax.dot_general(v_block, query.go[h], contract, preferred_element_type=jnp.float32)
    k_pos = k_first + lax.broadcasted_iota(jnp.int32, (k_block.shape[0], 1), 0)
    allowed = k_pos >= query.start
    if causal:
        allowed = allowed & (k_pos <= query.pos)
    prob = jnp.where(allowed, jnp.exp2(scores * (scaling * LOG2E) - query.norm[h]), 0.0)
    dscore = prob * (grads - query.delta[h]) * scaling
    return prob.astype(jnp.bfloat16), dscore.astype(jnp.bfloat16)


def fill(queries, blocks, firsts, causal, prob_ref, dscore_ref):
    for i, (block, first) in enumerate(zip(blocks, firsts)):
        rows, e = block.shape[0], block.shape[1] // 2
        part = pl.ds(i * rows, rows)
        k_block, v_block = block[:, :e], block[:, e:]
        column = 0
        for query in queries:
            for h in range(query.heads):
                prob, dscore = scores_block(query, h, k_block, v_block, first, causal)
                prob_ref[part, column : column + query.rows] = prob
                dscore_ref[part, column : column + query.rows] = dscore
                column += query.rows


def key_terms(queries, part, prob_ref, dscore_ref):
    go = jnp.concatenate([g for query in queries for g in query.go], axis=0)
    q = jnp.concatenate([g for query in queries for g in query.q], axis=0)
    dk = jnp.dot(dscore_ref[part, :], q, preferred_element_type=jnp.float32)
    dv = jnp.dot(prob_ref[part, :], go, preferred_element_type=jnp.float32)
    return jnp.concatenate([dk, dv], axis=1)


def query_terms(keys, dscore):
    return lax.dot_general(
        keys, dscore, (((0,), (0,)), ((), ())), preferred_element_type=jnp.float32
    )


def place():
    index = lax.axis_index("ctx")
    return index, index // 2, lax.rem(index, 2)


def near_core(chip):
    return (chip + 1) % 2


def behind(chip, core):
    return jnp.where(core == near_core(chip), 1, 2)


def block_start(chip, back, chips, rows):
    there = chip - back
    return jnp.where(there >= 0, there, -2 * chips) * (2 * rows)


def both_halves(pay_ref, heads, chip, core, rows, lens_ref):
    return [
        Query(pay_ref, half, heads, (2 * chip + half) * rows, lens_ref) for half in (core, 1 - core)
    ]


def own_kernel(heads, lens_ref, pay_ref, kv_ref, dqt_ref, dkv_ref, prob_ref, dscore_ref):
    rows, e = kv_ref.shape[0], kv_ref.shape[1] // 2
    index, chip, core = place()
    queries = both_halves(pay_ref, heads, chip, core, rows, lens_ref)
    fill(queries, [kv_ref[...]], [index * rows], True, prob_ref, dscore_ref)
    dkv_ref[...] = key_terms(queries, pl.ds(0, rows), prob_ref, dscore_ref)
    dqt = query_terms(kv_ref[:, :e], dscore_ref[...])
    for i in range(2):
        for h in range(heads):
            column = (i * heads + h) * rows
            dqt_ref[(i * heads + h) * e : (i * heads + h + 1) * e, :] = dqt[:, column : column + rows]


def near_kernel(
    heads, chips, lens_ref, own_ref, same_ref, dqt_in_ref, dqt_ref, dkv_ref, prob_ref, dscore_ref
):
    rows, e = same_ref.shape[0], same_ref.shape[1] // 2
    index, chip, core = place()
    own = both_halves(own_ref, heads, chip, core, rows, lens_ref)
    back = behind(chip, core)
    first = block_start(chip, back, chips, rows) + (back - 1) * rows
    fill(own, [same_ref[...]], [first], False, prob_ref, dscore_ref)
    dkv_ref[...] = key_terms(own, pl.ds(0, rows), prob_ref, dscore_ref)
    dqt = query_terms(same_ref[:, :e], dscore_ref[...])
    for i in range(2 * heads):
        block = pl.ds(i * e, e)
        dqt_ref[block, :] = dqt_in_ref[block, :] + dqt[:, i * rows : (i + 1) * rows]


def cross_kernel(
    heads, chips, lens_ref, own_ref, far_ref, same_ref, other_ref, dqt_in_ref, dkv_in_ref,
    dkv_ref, give_ref, keep_far_ref, keep_own_ref, prob_ref, dscore_ref
):
    rows, e = same_ref.shape[0], same_ref.shape[1] // 2
    index, chip, core = place()
    own = both_halves(own_ref, heads, chip, core, rows, lens_ref)
    far = both_halves(far_ref, heads, chip + 2, core, rows, lens_ref)
    for query in far:
        query.start = jnp.where(chip + 2 < chips, query.start, 4 * chips * rows)
    back = behind(chip, core)
    first = block_start(chip, back, chips, rows)
    half = 2 * heads * rows
    far_prob, far_dscore = prob_ref.at[:, half:], dscore_ref.at[:, half:]
    own_prob, own_dscore = prob_ref.at[rows:, :half], dscore_ref.at[rows:, :half]
    firsts = [first + (back - 1) * rows, first + (2 - back) * rows]
    fill(far, [same_ref[...], other_ref[...]], firsts, False, far_prob, far_dscore)
    fill(own, [other_ref[...]], firsts[1:], False, own_prob, own_dscore)
    terms = key_terms(far, pl.ds(0, 2 * rows), far_prob, far_dscore)
    same = terms[:rows] + dkv_in_ref[...]
    other = terms[rows:] + key_terms(own, pl.ds(0, rows), own_prob, own_dscore)
    dkv_ref[pl.ds(pl.multiple_of((back - 1) * rows, rows), rows), :] = same.astype(jnp.bfloat16)
    dkv_ref[pl.ds(pl.multiple_of((2 - back) * rows, rows), rows), :] = other.astype(jnp.bfloat16)
    keys = jnp.concatenate([same_ref[:, :e], other_ref[:, :e]], axis=0)
    dqt = query_terms(other_ref[:, :e], own_dscore[...])
    dqt_far = query_terms(keys, far_dscore[...])
    for i in range(2 * heads):
        columns = slice(i * rows, (i + 1) * rows)
        own_part = dqt_in_ref[i * e : (i + 1) * e, :] + dqt[:, columns]
        far_part = dqt_far[:, columns]
        if i < heads:
            block = pl.ds(i * e, e)
            keep_own_ref[block, :] = own_part
            keep_far_ref[block, :] = far_part
        else:
            give_ref[pl.ds((i - heads) * e, e), :] = far_part.astype(jnp.bfloat16)
            give_ref[pl.ds(i * e, e), :] = own_part.astype(jnp.bfloat16)


def pair_kernel(keep_ref, both_ref, send_ref):
    width = keep_ref.shape[0]
    _, _, core = place()
    other = both_ref[pl.ds(pl.multiple_of((1 - core) * 2 * width, width), width), :]
    send_ref[...] = (keep_ref[...] + other.astype(jnp.float32)).astype(jnp.bfloat16)


def final_kernel(keep_ref, both_ref, dkv_ref, back_ref, dqt_back_ref, dq_ref, dk_ref, dv_ref):
    width = keep_ref.shape[0]
    rows, e = dkv_ref.shape[0], dkv_ref.shape[1] // 2
    _, _, core = place()
    take = lambda ref, i, size: ref[pl.ds(pl.multiple_of(i * size, size), size), :].astype(jnp.float32)
    dqt = keep_ref[...] + take(both_ref, 2 * (1 - core) + 1, width)
    dq_ref[...] = (dqt + dqt_back_ref[...].astype(jnp.float32)).T.astype(jnp.bfloat16)
    total = dkv_ref[...] + take(back_ref, core, rows) + take(back_ref, 2 + core, rows)
    dk_ref[...] = total[:, :e].astype(jnp.bfloat16)
    dv_ref[...] = total[:, e:].astype(jnp.bfloat16)


def call(kernel, outs, name, flops=0, smem=0, space=pltpu.VMEM, scratch=()):
    def run(*args):
        specs = [pl.BlockSpec(memory_space=pltpu.SMEM)] * smem
        specs += [pl.BlockSpec(memory_space=space)] * (len(args) - smem)
        moved = sum(a.size * a.dtype.itemsize for a in args)
        return pl.pallas_call(
            kernel,
            out_shape=[jax.ShapeDtypeStruct(s, d) for s, d in outs],
            in_specs=specs,
            out_specs=[pl.BlockSpec(memory_space=pltpu.VMEM)] * len(outs),
            scratch_shapes=list(scratch),
            cost_estimate=pl.CostEstimate(flops=flops, bytes_accessed=moved, transcendentals=0),
            compiler_params=pltpu.CompilerParams(vmem_limit_bytes=32 * 1024 * 1024),
            name=name,
        )(*args)

    return run


def body(queries, key_states, value_states, attn_out, grad_out, log_norm, doc_lengths):
    rows, width = queries.shape
    heads = log_norm.shape[0]
    e = key_states.shape[1]
    count = lax.axis_size("ctx")
    chips = count // 2
    pairs = [[2 * i, 2 * i + 1] for i in range(chips)]
    bf16, f32 = jnp.bfloat16, jnp.float32

    def send(x, target):
        moves = [(i, target(i // 2, i % 2)) for i in range(count)]
        moves = [(i, 2 * chip + core) for i, (chip, core) in moves if 0 <= chip < chips]
        return lax.ppermute(x, "ctx", moves)

    def near(m):
        return (m + 1, near_core(m + 1))

    def far(m):
        return (m + 2, 1 - near_core(m + 2))

    def shift(x, by_even, by_odd, least=0):
        moves = [(i, i + (by_odd if i % 2 else by_even)) for i in range(count)]
        return lax.ppermute(x, "ctx", [(i, j) for i, j in moves if least <= i and least <= j < count])

    def pair_gather(x):
        return lax.all_gather(x, "ctx", axis=0, tiled=True, axis_index_groups=pairs)

    pay, kv = call(
        prep_kernel,
        [((2 * rows + STAT_ROWS, width), bf16), ((rows, 2 * e), bf16)],
        "prep",
        space=pltpu.HBM,
        scratch=[
            pltpu.VMEM((rows, width), bf16),
            pltpu.VMEM((heads, rows), f32),
            pltpu.SemaphoreType.DMA((6,)),
        ],
    )(
        *[
            pltpu.with_memory_space_constraint(x, pltpu.HBM)
            for x in (queries, grad_out, attn_out, log_norm, key_states, value_states)
        ]
    )
    pay_far = shift(pay, -4, -4, 2)
    kv_same = send(kv, lambda m, c: near(m) if c == 0 else far(m))
    kv_other = send(kv, lambda m, c: far(m) if c == 0 else near(m))
    pay_own = pair_gather(pay)
    unit = 5 * 2 * heads * rows * 2 * rows * e
    dqt, dkv_own = call(
        functools.partial(own_kernel, heads),
        [((2 * width, rows), f32), ((rows, 2 * e), f32)],
        "own",
        unit,
        1,
        scratch=[pltpu.VMEM((rows, 2 * heads * rows), bf16)] * 2,
    )(doc_lengths, pay_own, kv)
    dqt, dkv_same = call(
        functools.partial(near_kernel, heads, chips),
        [((2 * width, rows), f32), ((rows, 2 * e), f32)],
        "near",
        unit,
        1,
        scratch=[pltpu.VMEM((rows, 2 * heads * rows), bf16)] * 2,
    )(doc_lengths, pay_own, kv_same, dqt)
    pay_far, kv_other = lax.optimization_barrier((pay_far, kv_other))
    pay_ahead = pair_gather(pay_far)
    dkv, give, keep_far, keep_own = call(
        functools.partial(cross_kernel, heads, chips),
        [((2 * rows, 2 * e), bf16), ((2 * width, rows), bf16), ((width, rows), f32), ((width, rows), f32)],
        "cross",
        3 * unit,
        1,
        scratch=[pltpu.VMEM((2 * rows, 4 * heads * rows), bf16)] * 2,
    )(doc_lengths, pay_own, pay_ahead, kv_same, kv_other, dqt, dkv_same)
    dkv_back = send(
        dkv,
        lambda m, c: (m - 1, near_core(m - 1)) if c == near_core(m) else (m - 2, 1 - near_core(m - 2)),
    )
    both = pair_gather(give)
    (to_query,) = call(pair_kernel, [((width, rows), bf16)], "pair")(keep_far, both)
    dqt_back = shift(to_query, 4, 4, 2)
    back = pair_gather(dkv_back)
    grad_query, grad_key, grad_value = call(
        final_kernel, [((rows, width), bf16), ((rows, e), bf16), ((rows, e), bf16)], "final"
    )(keep_own, both, dkv_own, back, dqt_back)
    return (grad_query, grad_key, grad_value)


def solution(mesh):
    rows = P(("dp", "ctx"), None)
    placed = (rows, rows, rows, rows, rows, P(None, ("dp", "ctx")), P("dp"))
    return jax.shard_map(
        body, mesh=mesh, in_specs=placed, out_specs=(rows, rows, rows), check_vma=False
    )
```

```python
import functools
import math

import jax
import jax.numpy as jnp
from jax import lax
from jax.experimental import pallas as pl
from jax.experimental.pallas import tpu as pltpu
from jax.sharding import PartitionSpec as P

LOG2E = math.log2(math.e)
STAT_ROWS = 16


def split3(value):
    high = value.astype(jnp.bfloat16)
    rest = value - high.astype(jnp.float32)
    mid = rest.astype(jnp.bfloat16)
    low = (rest - mid.astype(jnp.float32)).astype(jnp.bfloat16)
    return high, mid, low


def prep_kernel(q_ref, go_ref, out_ref, norm_ref, k_ref, v_ref, pay_ref, kv_ref, *scratch):
    out_buf, norm_buf, sems = scratch
    rows, width = q_ref.shape
    heads = norm_ref.shape[0]
    e = width // heads
    moves = [
        (go_ref, pay_ref.at[rows : 2 * rows]),
        (out_ref, out_buf),
        (norm_ref, norm_buf),
        (q_ref, pay_ref.at[:rows]),
        (k_ref, kv_ref.at[:, :e]),
        (v_ref, kv_ref.at[:, e:]),
    ]
    copies = [pltpu.make_async_copy(s, d, sems.at[i]) for i, (s, d) in enumerate(moves)]
    for copy in copies:
        copy.start()
    for copy in copies[:3]:
        copy.wait()
    product = pay_ref[rows : 2 * rows].astype(jnp.float32) * out_buf[...].astype(jnp.float32)
    product_t = product.T
    stats = []
    for h in range(heads):
        delta = jnp.sum(product_t[h * e : (h + 1) * e], axis=0, keepdims=True)
        stats += list(split3(norm_buf[h : h + 1, :] * LOG2E)) + list(split3(delta))
    stats += [jnp.zeros((1, rows), jnp.bfloat16)] * (STAT_ROWS - len(stats))
    table = jnp.concatenate([s.astype(jnp.float32) for s in stats], axis=0)
    pay_ref[2 * rows :, :rows] = table.astype(jnp.bfloat16)
    for copy in copies[3:]:
        copy.wait()


class Query:
    def __init__(self, pay_ref, block, heads, first, lens_ref):
        rows, width = (pay_ref.shape[0] // 2 - STAT_ROWS) // 2, pay_ref.shape[1]
        e = width // heads
        base = block * (2 * rows + STAT_ROWS)
        self.heads, self.rows, self.e = heads, rows, e
        part = lambda at, size: pl.ds(pl.multiple_of(base + at, STAT_ROWS), size)
        self.q = [pay_ref[part(0, rows), h * e : (h + 1) * e] for h in range(heads)]
        self.go = [pay_ref[part(rows, rows), h * e : (h + 1) * e] for h in range(heads)]
        table = pay_ref[part(2 * rows, STAT_ROWS), :rows].astype(jnp.float32)
        row = lambda i: table[i : i + 1]
        self.norm = [row(6 * h) + row(6 * h + 1) + row(6 * h + 2) for h in range(heads)]
        self.delta = [row(6 * h + 3) + row(6 * h + 4) + row(6 * h + 5) for h in range(heads)]
        self.pos = first + lax.broadcasted_iota(jnp.int32, (1, rows), 1)
        self.start = jnp.zeros((1, rows), jnp.int32)
        end = jnp.int32(0)
        for d in range(lens_ref.shape[0]):
            end = end + lens_ref[d]
            self.start = jnp.where(end <= self.pos, end, self.start)


def scores_block(query, h, k_block, v_block, k_first, causal):
    contract = (((1,), (1,)), ((), ()))
    scaling = query.e ** (-0.5)
    scores = lax.dot_general(k_block, query.q[h], contract, preferred_element_type=jnp.float32)
    grads = lax.dot_general(v_block, query.go[h], contract, preferred_element_type=jnp.float32)
    k_pos = k_first + lax.broadcasted_iota(jnp.int32, (k_block.shape[0], 1), 0)
    allowed = k_pos >= query.start
    if causal:
        allowed = allowed & (k_pos <= query.pos)
    prob = jnp.where(allowed, jnp.exp2(scores * (scaling * LOG2E) - query.norm[h]), 0.0)
    dscore = prob * (grads - query.delta[h]) * scaling
    return prob.astype(jnp.bfloat16), dscore.astype(jnp.bfloat16)


def fill(queries, blocks, firsts, causal, prob_ref, dscore_ref):
    for i, (block, first) in enumerate(zip(blocks, firsts)):
        rows, e = block.shape[0], block.shape[1] // 2
        part = pl.ds(i * rows, rows)
        k_block, v_block = block[:, :e], block[:, e:]
        column = 0
        for query in queries:
            for h in range(query.heads):
                prob, dscore = scores_block(query, h, k_block, v_block, first, causal)
                prob_ref[part, column : column + query.rows] = prob
                dscore_ref[part, column : column + query.rows] = dscore
                column += query.rows


def key_terms(queries, part, prob_ref, dscore_ref):
    go = jnp.concatenate([g for query in queries for g in query.go], axis=0)
    q = jnp.concatenate([g for query in queries for g in query.q], axis=0)
    dk = jnp.dot(dscore_ref[part, :], q, preferred_element_type=jnp.float32)
    dv = jnp.dot(prob_ref[part, :], go, preferred_element_type=jnp.float32)
    return jnp.concatenate([dk, dv], axis=1)


def query_terms(keys, dscore):
    return lax.dot_general(
        keys, dscore, (((0,), (0,)), ((), ())), preferred_element_type=jnp.float32
    )


def place():
    index = lax.axis_index("ctx")
    return index, index // 2, lax.rem(index, 2)


def near_core(chip):
    return (chip + 1) % 2


def behind(chip, core):
    return jnp.where(core == near_core(chip), 1, 2)


def block_start(chip, back, chips, rows):
    there = chip - back
    return jnp.where(there >= 0, there, -2 * chips) * (2 * rows)


def both_halves(pay_ref, heads, chip, core, rows, lens_ref):
    return [
        Query(pay_ref, half, heads, (2 * chip + half) * rows, lens_ref) for half in (core, 1 - core)
    ]


def own_kernel(heads, lens_ref, pay_ref, kv_ref, dqt_ref, dkv_ref, prob_ref, dscore_ref):
    rows, e = kv_ref.shape[0], kv_ref.shape[1] // 2
    index, chip, core = place()
    queries = both_halves(pay_ref, heads, chip, core, rows, lens_ref)
    fill(queries, [kv_ref[...]], [index * rows], True, prob_ref, dscore_ref)
    dkv_ref[...] = key_terms(queries, pl.ds(0, rows), prob_ref, dscore_ref)
    dqt = query_terms(kv_ref[:, :e], dscore_ref[...])
    for i in range(2):
        for h in range(heads):
            column = (i * heads + h) * rows
            dqt_ref[(i * heads + h) * e : (i * heads + h + 1) * e, :] = dqt[:, column : column + rows]


def near_kernel(
    heads, chips, lens_ref, own_ref, same_ref, dqt_in_ref, dqt_ref, dkv_ref, prob_ref, dscore_ref
):
    rows, e = same_ref.shape[0], same_ref.shape[1] // 2
    index, chip, core = place()
    own = both_halves(own_ref, heads, chip, core, rows, lens_ref)
    back = behind(chip, core)
    first = block_start(chip, back, chips, rows) + (2 - back) * rows
    fill(own, [same_ref[...]], [first], False, prob_ref, dscore_ref)
    dkv_ref[...] = key_terms(own, pl.ds(0, rows), prob_ref, dscore_ref)
    dqt = query_terms(same_ref[:, :e], dscore_ref[...])
    for i in range(2 * heads):
        block = pl.ds(i * e, e)
        dqt_ref[block, :] = dqt_in_ref[block, :] + dqt[:, i * rows : (i + 1) * rows]


def cross_kernel(
    heads, chips, lens_ref, own_ref, far_ref, same_ref, other_ref, dqt_in_ref, dkv_in_ref,
    dkv_ref, give_ref, keep_far_ref, keep_own_ref, prob_ref, dscore_ref
):
    rows, e = same_ref.shape[0], same_ref.shape[1] // 2
    index, chip, core = place()
    own = both_halves(own_ref, heads, chip, core, rows, lens_ref)
    far = both_halves(far_ref, heads, chip + 2, core, rows, lens_ref)
    for query in far:
        query.start = jnp.where(chip + 2 < chips, query.start, 4 * chips * rows)
    back = behind(chip, core)
    first = block_start(chip, back, chips, rows)
    half = 2 * heads * rows
    far_prob, far_dscore = prob_ref.at[:, half:], dscore_ref.at[:, half:]
    own_prob, own_dscore = prob_ref.at[rows:, :half], dscore_ref.at[rows:, :half]
    firsts = [first + (2 - back) * rows, first + (back - 1) * rows]
    fill(far, [same_ref[...], other_ref[...]], firsts, False, far_prob, far_dscore)
    fill(own, [other_ref[...]], firsts[1:], False, own_prob, own_dscore)
    terms = key_terms(far, pl.ds(0, 2 * rows), far_prob, far_dscore)
    same = terms[:rows] + dkv_in_ref[...]
    other = terms[rows:] + key_terms(own, pl.ds(0, rows), own_prob, own_dscore)
    dkv_ref[pl.ds(pl.multiple_of((2 - back) * rows, rows), rows), :] = same.astype(jnp.bfloat16)
    dkv_ref[pl.ds(pl.multiple_of((back - 1) * rows, rows), rows), :] = other.astype(jnp.bfloat16)
    keys = jnp.concatenate([same_ref[:, :e], other_ref[:, :e]], axis=0)
    dqt = query_terms(other_ref[:, :e], own_dscore[...])
    dqt_far = query_terms(keys, far_dscore[...])
    for i in range(2 * heads):
        columns = slice(i * rows, (i + 1) * rows)
        own_part = dqt_in_ref[i * e : (i + 1) * e, :] + dqt[:, columns]
        far_part = dqt_far[:, columns]
        if i < heads:
            block = pl.ds(i * e, e)
            keep_own_ref[block, :] = own_part
            keep_far_ref[block, :] = far_part
        else:
            give_ref[pl.ds((i - heads) * e, e), :] = far_part.astype(jnp.bfloat16)
            give_ref[pl.ds(i * e, e), :] = own_part.astype(jnp.bfloat16)


def pair_kernel(keep_ref, both_ref, send_ref):
    width = keep_ref.shape[0]
    _, _, core = place()
    other = both_ref[pl.ds(pl.multiple_of((1 - core) * 2 * width, width), width), :]
    send_ref[...] = (keep_ref[...] + other.astype(jnp.float32)).astype(jnp.bfloat16)


def final_kernel(keep_ref, both_ref, dkv_ref, back_ref, dqt_back_ref, dq_ref, dk_ref, dv_ref):
    width = keep_ref.shape[0]
    rows, e = dkv_ref.shape[0], dkv_ref.shape[1] // 2
    _, _, core = place()
    take = lambda ref, i, size: ref[pl.ds(pl.multiple_of(i * size, size), size), :].astype(jnp.float32)
    dqt = keep_ref[...] + take(both_ref, 2 * (1 - core) + 1, width)
    dq_ref[...] = (dqt + dqt_back_ref[...].astype(jnp.float32)).T.astype(jnp.bfloat16)
    total = dkv_ref[...] + take(back_ref, core, rows) + take(back_ref, 2 + core, rows)
    dk_ref[...] = total[:, :e].astype(jnp.bfloat16)
    dv_ref[...] = total[:, e:].astype(jnp.bfloat16)


def call(kernel, outs, name, flops=0, smem=0, space=pltpu.VMEM, scratch=()):
    def run(*args):
        specs = [pl.BlockSpec(memory_space=pltpu.SMEM)] * smem
        specs += [pl.BlockSpec(memory_space=space)] * (len(args) - smem)
        moved = sum(a.size * a.dtype.itemsize for a in args)
        return pl.pallas_call(
            kernel,
            out_shape=[jax.ShapeDtypeStruct(s, d) for s, d in outs],
            in_specs=specs,
            out_specs=[pl.BlockSpec(memory_space=pltpu.VMEM)] * len(outs),
            scratch_shapes=list(scratch),
            cost_estimate=pl.CostEstimate(flops=flops, bytes_accessed=moved, transcendentals=0),
            compiler_params=pltpu.CompilerParams(vmem_limit_bytes=32 * 1024 * 1024),
            name=name,
        )(*args)

    return run


def body(queries, key_states, value_states, attn_out, grad_out, log_norm, doc_lengths):
    rows, width = queries.shape
    heads = log_norm.shape[0]
    e = key_states.shape[1]
    count = lax.axis_size("ctx")
    chips = count // 2
    pairs = [[2 * i, 2 * i + 1] for i in range(chips)]
    bf16, f32 = jnp.bfloat16, jnp.float32

    def send(x, target):
        moves = [(i, target(i // 2, i % 2)) for i in range(count)]
        moves = [(i, 2 * chip + core) for i, (chip, core) in moves if 0 <= chip < chips]
        return lax.ppermute(x, "ctx", moves)

    def near(m):
        return (m + 1, near_core(m + 1))

    def far(m):
        return (m + 2, 1 - near_core(m + 2))

    def shift(x, by_even, by_odd, least=0):
        moves = [(i, i + (by_odd if i % 2 else by_even)) for i in range(count)]
        return lax.ppermute(x, "ctx", [(i, j) for i, j in moves if least <= i and least <= j < count])

    def pair_gather(x):
        return lax.all_gather(x, "ctx", axis=0, tiled=True, axis_index_groups=pairs)

    pay, kv = call(
        prep_kernel,
        [((2 * rows + STAT_ROWS, width), bf16), ((rows, 2 * e), bf16)],
        "prep",
        space=pltpu.HBM,
        scratch=[
            pltpu.VMEM((rows, width), bf16),
            pltpu.VMEM((heads, rows), f32),
            pltpu.SemaphoreType.DMA((6,)),
        ],
    )(
        *[
            pltpu.with_memory_space_constraint(x, pltpu.HBM)
            for x in (queries, grad_out, attn_out, log_norm, key_states, value_states)
        ]
    )
    pay_far = shift(pay, -4, -4, 2)
    kv_same = send(kv, lambda m, c: near(m) if c == 1 else far(m))
    kv_other = send(kv, lambda m, c: far(m) if c == 1 else near(m))
    pay_own = pair_gather(pay)
    unit = 5 * 2 * heads * rows * 2 * rows * e
    dqt, dkv_own = call(
        functools.partial(own_kernel, heads),
        [((2 * width, rows), f32), ((rows, 2 * e), f32)],
        "own",
        unit,
        1,
        scratch=[pltpu.VMEM((rows, 2 * heads * rows), bf16)] * 2,
    )(doc_lengths, pay_own, kv)
    dqt, dkv_same = call(
        functools.partial(near_kernel, heads, chips),
        [((2 * width, rows), f32), ((rows, 2 * e), f32)],
        "near",
        unit,
        1,
        scratch=[pltpu.VMEM((rows, 2 * heads * rows), bf16)] * 2,
    )(doc_lengths, pay_own, kv_same, dqt)
    pay_far, kv_other = lax.optimization_barrier((pay_far, kv_other))
    pay_ahead = pair_gather(pay_far)
    dkv, give, keep_far, keep_own = call(
        functools.partial(cross_kernel, heads, chips),
        [((2 * rows, 2 * e), bf16), ((2 * width, rows), bf16), ((width, rows), f32), ((width, rows), f32)],
        "cross",
        3 * unit,
        1,
        scratch=[pltpu.VMEM((2 * rows, 4 * heads * rows), bf16)] * 2,
    )(doc_lengths, pay_own, pay_ahead, kv_same, kv_other, dqt, dkv_same)
    dkv_back = send(
        dkv,
        lambda m, c: (m - 1, near_core(m - 1)) if c == near_core(m) else (m - 2, 1 - near_core(m - 2)),
    )
    both = pair_gather(give)
    (to_query,) = call(pair_kernel, [((width, rows), bf16)], "pair")(keep_far, both)
    dqt_back = shift(to_query, 4, 4, 2)
    back = pair_gather(dkv_back)
    grad_query, grad_key, grad_value = call(
        final_kernel, [((rows, width), bf16), ((rows, e), bf16), ((rows, e), bf16)], "final"
    )(keep_own, both, dkv_own, back, dqt_back)
    return (grad_query, grad_key, grad_value)


def solution(mesh):
    rows = P(("dp", "ctx"), None)
    placed = (rows, rows, rows, rows, rows, P(None, ("dp", "ctx")), P("dp"))
    return jax.shard_map(
        body, mesh=mesh, in_specs=placed, out_specs=(rows, rows, rows), check_vma=False
    )
```

```python
import functools
import math

import jax
import jax.numpy as jnp
from jax import lax
from jax.experimental import pallas as pl
from jax.experimental.pallas import tpu as pltpu
from jax.sharding import PartitionSpec as P

LOG2E = math.log2(math.e)
STAT_ROWS = 16


def split3(value):
    high = value.astype(jnp.bfloat16)
    rest = value - high.astype(jnp.float32)
    mid = rest.astype(jnp.bfloat16)
    low = (rest - mid.astype(jnp.float32)).astype(jnp.bfloat16)
    return high, mid, low


def prep_kernel(q_ref, go_ref, out_ref, norm_ref, k_ref, v_ref, pay_ref, kv_ref, *scratch):
    out_buf, norm_buf, sems = scratch
    rows, width = q_ref.shape
    heads = norm_ref.shape[0]
    e = width // heads
    moves = [
        (go_ref, pay_ref.at[rows : 2 * rows]),
        (out_ref, out_buf),
        (norm_ref, norm_buf),
        (q_ref, pay_ref.at[:rows]),
        (k_ref, kv_ref.at[:, :e]),
        (v_ref, kv_ref.at[:, e:]),
    ]
    copies = [pltpu.make_async_copy(s, d, sems.at[i]) for i, (s, d) in enumerate(moves)]
    for copy in copies:
        copy.start()
    for copy in copies[:3]:
        copy.wait()
    product = pay_ref[rows : 2 * rows].astype(jnp.float32) * out_buf[...].astype(jnp.float32)
    product_t = product.T
    stats = []
    for h in range(heads):
        delta = jnp.sum(product_t[h * e : (h + 1) * e], axis=0, keepdims=True)
        stats += list(split3(norm_buf[h : h + 1, :] * LOG2E)) + list(split3(delta))
    stats += [jnp.zeros((1, rows), jnp.bfloat16)] * (STAT_ROWS - len(stats))
    table = jnp.concatenate([s.astype(jnp.float32) for s in stats], axis=0)
    pay_ref[2 * rows :, :rows] = table.astype(jnp.bfloat16)
    for copy in copies[3:]:
        copy.wait()


class Query:
    def __init__(self, pay_ref, block, heads, first, lens_ref):
        rows, width = (pay_ref.shape[0] // 2 - STAT_ROWS) // 2, pay_ref.shape[1]
        e = width // heads
        base = block * (2 * rows + STAT_ROWS)
        self.heads, self.rows, self.e = heads, rows, e
        part = lambda at, size: pl.ds(pl.multiple_of(base + at, STAT_ROWS), size)
        self.q = [pay_ref[part(0, rows), h * e : (h + 1) * e] for h in range(heads)]
        self.go = [pay_ref[part(rows, rows), h * e : (h + 1) * e] for h in range(heads)]
        table = pay_ref[part(2 * rows, STAT_ROWS), :rows].astype(jnp.float32)
        row = lambda i: table[i : i + 1]
        self.norm = [row(6 * h) + row(6 * h + 1) + row(6 * h + 2) for h in range(heads)]
        self.delta = [row(6 * h + 3) + row(6 * h + 4) + row(6 * h + 5) for h in range(heads)]
        self.pos = first + lax.broadcasted_iota(jnp.int32, (1, rows), 1)
        self.start = jnp.zeros((1, rows), jnp.int32)
        end = jnp.int32(0)
        for d in range(lens_ref.shape[0]):
            end = end + lens_ref[d]
            self.start = jnp.where(end <= self.pos, end, self.start)


def scores_block(query, h, k_block, v_block, k_first, causal):
    contract = (((1,), (1,)), ((), ()))
    scaling = query.e ** (-0.5)
    scores = lax.dot_general(k_block, query.q[h], contract, preferred_element_type=jnp.float32)
    grads = lax.dot_general(v_block, query.go[h], contract, preferred_element_type=jnp.float32)
    k_pos = k_first + lax.broadcasted_iota(jnp.int32, (k_block.shape[0], 1), 0)
    allowed = k_pos >= query.start
    if causal:
        allowed = allowed & (k_pos <= query.pos)
    prob = jnp.where(allowed, jnp.exp2(scores * (scaling * LOG2E) - query.norm[h]), 0.0)
    dscore = prob * (grads - query.delta[h]) * scaling
    return prob.astype(jnp.bfloat16), dscore.astype(jnp.bfloat16)


def fill(queries, blocks, firsts, causal, prob_ref, dscore_ref):
    for i, (block, first) in enumerate(zip(blocks, firsts)):
        rows, e = block.shape[0], block.shape[1] // 2
        part = pl.ds(i * rows, rows)
        k_block, v_block = block[:, :e], block[:, e:]
        column = 0
        for query in queries:
            for h in range(query.heads):
                prob, dscore = scores_block(query, h, k_block, v_block, first, causal)
                prob_ref[part, column : column + query.rows] = prob
                dscore_ref[part, column : column + query.rows] = dscore
                column += query.rows


def key_terms(queries, part, prob_ref, dscore_ref):
    go = jnp.concatenate([g for query in queries for g in query.go], axis=0)
    q = jnp.concatenate([g for query in queries for g in query.q], axis=0)
    dk = jnp.dot(dscore_ref[part, :], q, preferred_element_type=jnp.float32)
    dv = jnp.dot(prob_ref[part, :], go, preferred_element_type=jnp.float32)
    return jnp.concatenate([dk, dv], axis=1)


def query_terms(keys, dscore):
    return lax.dot_general(
        keys, dscore, (((0,), (0,)), ((), ())), preferred_element_type=jnp.float32
    )


def place():
    index = lax.axis_index("ctx")
    return index, index // 2, lax.rem(index, 2)


def near_core(chip):
    return (chip + 1) % 2


def behind(chip, core):
    return jnp.where(core == near_core(chip), 1, 2)


def block_start(chip, back, chips, rows):
    there = chip - back
    return jnp.where(there >= 0, there, -2 * chips) * (2 * rows)


def both_halves(pay_ref, heads, chip, core, rows, lens_ref):
    return [
        Query(pay_ref, half, heads, (2 * chip + half) * rows, lens_ref) for half in (core, 1 - core)
    ]


def own_kernel(heads, lens_ref, pay_ref, kv_ref, dqt_ref, dkv_ref, prob_ref, dscore_ref):
    rows, e = kv_ref.shape[0], kv_ref.shape[1] // 2
    index, chip, core = place()
    queries = both_halves(pay_ref, heads, chip, core, rows, lens_ref)
    fill(queries, [kv_ref[...]], [index * rows], True, prob_ref, dscore_ref)
    dkv_ref[...] = key_terms(queries, pl.ds(0, rows), prob_ref, dscore_ref)
    dqt = query_terms(kv_ref[:, :e], dscore_ref[...])
    for i in range(2):
        for h in range(heads):
            column = (i * heads + h) * rows
            dqt_ref[(i * heads + h) * e : (i * heads + h + 1) * e, :] = dqt[:, column : column + rows]


def near_kernel(
    heads, chips, lens_ref, own_ref, same_ref, dqt_in_ref, dqt_ref, dkv_ref, prob_ref, dscore_ref
):
    rows, e = same_ref.shape[0], same_ref.shape[1] // 2
    index, chip, core = place()
    own = both_halves(own_ref, heads, chip, core, rows, lens_ref)
    back = behind(chip, core)
    first = block_start(chip, back, chips, rows) + (2 - back) * rows
    fill(own, [same_ref[...]], [first], False, prob_ref, dscore_ref)
    dkv_ref[...] = key_terms(own, pl.ds(0, rows), prob_ref, dscore_ref)
    dqt = query_terms(same_ref[:, :e], dscore_ref[...])
    for i in range(2 * heads):
        block = pl.ds(i * e, e)
        dqt_ref[block, :] = dqt_in_ref[block, :] + dqt[:, i * rows : (i + 1) * rows]


def cross_kernel(
    heads, chips, lens_ref, own_ref, far_ref, same_ref, other_ref, dqt_in_ref, dkv_in_ref,
    dkv_ref, give_ref, keep_far_ref, keep_own_ref, prob_ref, dscore_ref
):
    rows, e = same_ref.shape[0], same_ref.shape[1] // 2
    index, chip, core = place()
    own = both_halves(own_ref, heads, chip, core, rows, lens_ref)
    far = both_halves(far_ref, heads, chip + 2, core, rows, lens_ref)
    for query in far:
        query.start = jnp.where(chip + 2 < chips, query.start, 4 * chips * rows)
    back = behind(chip, core)
    first = block_start(chip, back, chips, rows)
    half = 2 * heads * rows
    far_prob, far_dscore = prob_ref.at[:, half:], dscore_ref.at[:, half:]
    own_prob, own_dscore = prob_ref.at[rows:, :half], dscore_ref.at[rows:, :half]
    firsts = [first + (2 - back) * rows, first + (back - 1) * rows]
    fill(own, [other_ref[...]], firsts[1:], False, own_prob, own_dscore)
    fill(far, [same_ref[...], other_ref[...]], firsts, False, far_prob, far_dscore)
    own_terms = key_terms(own, pl.ds(0, rows), own_prob, own_dscore)
    terms = key_terms(far, pl.ds(0, 2 * rows), far_prob, far_dscore)
    same = terms[:rows] + dkv_in_ref[...]
    other = terms[rows:] + own_terms
    dkv_ref[pl.ds(pl.multiple_of((2 - back) * rows, rows), rows), :] = same.astype(jnp.bfloat16)
    dkv_ref[pl.ds(pl.multiple_of((back - 1) * rows, rows), rows), :] = other.astype(jnp.bfloat16)
    keys = jnp.concatenate([same_ref[:, :e], other_ref[:, :e]], axis=0)
    dqt = query_terms(other_ref[:, :e], own_dscore[...])
    dqt_far = query_terms(keys, far_dscore[...])
    for i in range(2 * heads):
        columns = slice(i * rows, (i + 1) * rows)
        own_part = dqt_in_ref[i * e : (i + 1) * e, :] + dqt[:, columns]
        far_part = dqt_far[:, columns]
        if i < heads:
            block = pl.ds(i * e, e)
            keep_own_ref[block, :] = own_part
            keep_far_ref[block, :] = far_part
        else:
            give_ref[pl.ds((i - heads) * e, e), :] = far_part.astype(jnp.bfloat16)
            give_ref[pl.ds(i * e, e), :] = own_part.astype(jnp.bfloat16)


def pair_kernel(keep_ref, both_ref, send_ref):
    width = keep_ref.shape[0]
    _, _, core = place()
    other = both_ref[pl.ds(pl.multiple_of((1 - core) * 2 * width, width), width), :]
    send_ref[...] = (keep_ref[...] + other.astype(jnp.float32)).astype(jnp.bfloat16)


def final_kernel(keep_ref, both_ref, dkv_ref, back_ref, dqt_back_ref, dq_ref, dk_ref, dv_ref):
    width = keep_ref.shape[0]
    rows, e = dkv_ref.shape[0], dkv_ref.shape[1] // 2
    _, _, core = place()
    take = lambda ref, i, size: ref[pl.ds(pl.multiple_of(i * size, size), size), :].astype(jnp.float32)
    dqt = keep_ref[...] + take(both_ref, 2 * (1 - core) + 1, width)
    dq_ref[...] = (dqt + dqt_back_ref[...].astype(jnp.float32)).T.astype(jnp.bfloat16)
    total = dkv_ref[...] + take(back_ref, core, rows) + take(back_ref, 2 + core, rows)
    dk_ref[...] = total[:, :e].astype(jnp.bfloat16)
    dv_ref[...] = total[:, e:].astype(jnp.bfloat16)


def call(kernel, outs, name, flops=0, smem=0, space=pltpu.VMEM, scratch=()):
    def run(*args):
        specs = [pl.BlockSpec(memory_space=pltpu.SMEM)] * smem
        specs += [pl.BlockSpec(memory_space=space)] * (len(args) - smem)
        moved = sum(a.size * a.dtype.itemsize for a in args)
        return pl.pallas_call(
            kernel,
            out_shape=[jax.ShapeDtypeStruct(s, d) for s, d in outs],
            in_specs=specs,
            out_specs=[pl.BlockSpec(memory_space=pltpu.VMEM)] * len(outs),
            scratch_shapes=list(scratch),
            cost_estimate=pl.CostEstimate(flops=flops, bytes_accessed=moved, transcendentals=0),
            compiler_params=pltpu.CompilerParams(vmem_limit_bytes=32 * 1024 * 1024),
            name=name,
        )(*args)

    return run


def body(queries, key_states, value_states, attn_out, grad_out, log_norm, doc_lengths):
    rows, width = queries.shape
    heads = log_norm.shape[0]
    e = key_states.shape[1]
    count = lax.axis_size("ctx")
    chips = count // 2
    pairs = [[2 * i, 2 * i + 1] for i in range(chips)]
    bf16, f32 = jnp.bfloat16, jnp.float32

    def send(x, target):
        moves = [(i, target(i // 2, i % 2)) for i in range(count)]
        moves = [(i, 2 * chip + core) for i, (chip, core) in moves if 0 <= chip < chips]
        return lax.ppermute(x, "ctx", moves)

    def near(m):
        return (m + 1, near_core(m + 1))

    def far(m):
        return (m + 2, 1 - near_core(m + 2))

    def shift(x, by_even, by_odd, least=0):
        moves = [(i, i + (by_odd if i % 2 else by_even)) for i in range(count)]
        return lax.ppermute(x, "ctx", [(i, j) for i, j in moves if least <= i and least <= j < count])

    def pair_gather(x):
        return lax.all_gather(x, "ctx", axis=0, tiled=True, axis_index_groups=pairs)

    pay, kv = call(
        prep_kernel,
        [((2 * rows + STAT_ROWS, width), bf16), ((rows, 2 * e), bf16)],
        "prep",
        space=pltpu.HBM,
        scratch=[
            pltpu.VMEM((rows, width), bf16),
            pltpu.VMEM((heads, rows), f32),
            pltpu.SemaphoreType.DMA((6,)),
        ],
    )(
        *[
            pltpu.with_memory_space_constraint(x, pltpu.HBM)
            for x in (queries, grad_out, attn_out, log_norm, key_states, value_states)
        ]
    )
    pay_far = shift(pay, -4, -4, 2)
    kv_same = send(kv, lambda m, c: near(m) if c == 1 else far(m))
    kv_other = send(kv, lambda m, c: far(m) if c == 1 else near(m))
    pay_own = pair_gather(pay)
    unit = 5 * 2 * heads * rows * 2 * rows * e
    dqt, dkv_own = call(
        functools.partial(own_kernel, heads),
        [((2 * width, rows), f32), ((rows, 2 * e), f32)],
        "own",
        unit,
        1,
        scratch=[pltpu.VMEM((rows, 2 * heads * rows), bf16)] * 2,
    )(doc_lengths, pay_own, kv)
    dqt, dkv_same = call(
        functools.partial(near_kernel, heads, chips),
        [((2 * width, rows), f32), ((rows, 2 * e), f32)],
        "near",
        unit,
        1,
        scratch=[pltpu.VMEM((rows, 2 * heads * rows), bf16)] * 2,
    )(doc_lengths, pay_own, kv_same, dqt)
    pay_far, kv_other = lax.optimization_barrier((pay_far, kv_other))
    pay_ahead = pair_gather(pay_far)
    dkv, give, keep_far, keep_own = call(
        functools.partial(cross_kernel, heads, chips),
        [((2 * rows, 2 * e), bf16), ((2 * width, rows), bf16), ((width, rows), f32), ((width, rows), f32)],
        "cross",
        3 * unit,
        1,
        scratch=[pltpu.VMEM((2 * rows, 4 * heads * rows), bf16)] * 2,
    )(doc_lengths, pay_own, pay_ahead, kv_same, kv_other, dqt, dkv_same)
    dkv_back = send(
        dkv,
        lambda m, c: (m - 1, near_core(m - 1)) if c == near_core(m) else (m - 2, 1 - near_core(m - 2)),
    )
    both = pair_gather(give)
    (to_query,) = call(pair_kernel, [((width, rows), bf16)], "pair")(keep_far, both)
    dqt_back = shift(to_query, 4, 4, 2)
    back = pair_gather(dkv_back)
    grad_query, grad_key, grad_value = call(
        final_kernel, [((rows, width), bf16), ((rows, e), bf16), ((rows, e), bf16)], "final"
    )(keep_own, both, dkv_own, back, dqt_back)
    return (grad_query, grad_key, grad_value)


def solution(mesh):
    rows = P(("dp", "ctx"), None)
    placed = (rows, rows, rows, rows, rows, P(None, ("dp", "ctx")), P("dp"))
    return jax.shard_map(
        body, mesh=mesh, in_specs=placed, out_specs=(rows, rows, rows), check_vma=False
    )
```
